128 devices in a mesh: lon: 16 (over y_hi, x, core), lat: 8 (over y_lo, z).
Axes of the slice: x: 4, y: 4 (y_hi: 2, y_lo: 2; y = y_hi * 2 + y_lo), z: 4, core: 2. Of those that a mesh axis runs over, the one named last changes fastest.
Arguments:
- tokens: bfloat16 [4, 48, 768, 192], P(None, 'lat', 'lon'), may hold values from -6 to 6
- norm1_gain: float32 [192], replicated, may hold values from 0.1 to 1.9
- w_qkv: bfloat16 [192, 576], replicated, may hold values from -0.4375 to 0.4375
- w_proj: bfloat16 [192, 192], replicated, may hold values from -0.4375 to 0.4375
- bias_table: float32 [2, 8, 6, 3312], P(None, 'lat'), may hold values from -4 to 4
- pos_index: int32 [144, 144], replicated, may hold values from 0 to 3311, as said below
- mask_ids: int32 [48], P('lat'), may hold values from 0 to 7, never falling along the last dimension, each value on 1 to 12 neighbouring positions
- norm2_gain: float32 [192], replicated, may hold values from 0.1 to 1.9
- w_fc1: bfloat16 [192, 768], replicated, may hold values from -0.4375 to 0.4375
- w_fc2: bfloat16 [768, 192], replicated, may hold values from -0.21875 to 0.21875
- cotangent: bfloat16 [4, 48, 768, 192], P(None, 'lat', 'lon'), may hold values from -6 to 6
Outputs:
- block_out: bfloat16 [4, 48, 768, 192], P(None, 'lat', 'lon')
- grad_tokens: bfloat16 [4, 48, 768, 192], P(None, 'lat', 'lon')
- grad_norm1: float32 [192], replicated
- grad_qkv: float32 [192, 576], replicated
- grad_proj: float32 [192, 192], replicated
- grad_table: float32 [2, 8, 6, 3312], P(None, 'lat')
- grad_norm2: float32 [192], replicated
- grad_fc1: float32 [192, 768], replicated
- grad_fc2: float32 [768, 192], replicated
The draws below stay inside these ranges and needn't reach their ends.
Inputs may be any that keep to these rules, and one draw needn't show every extreme that they name: pos_index[i, j] depends only on the level pair, the row pair and the column offset of tokens i and j of a window, and distinct such triples have distinct entries. mask_ids never falls along latitude; a region holds at most 12 rows.
All inputs are finite; a program needn't handle non-finite values.
Results may differ from the reference program's by a relative error of at most 0.023.
Values may be sent and summed in bfloat16 or wider, within the bound.
A program may use at most 128 MiB of HBM per device.

```python
import math
import jax
import jax.numpy as jnp
import numpy as np
from jax import lax

C = 192
HEADS = 6
FFN = 768
WZ = 2
WH = 6
WW = 12
POS = 3312
LEVELS = 4
ZWIN = 2
NLAT = 48
NLON = 768
LATWIN = 8
TOKENS = 147456


def draw_pos_index(key, part):
    key = jax.random.fold_in(key, 11)
    order = jax.random.permutation(key, WZ * WZ * WH * WH * (2 * WW - 1))
    token_ids = jnp.arange(WZ * WH * WW)
    level_of = token_ids // (WH * WW)
    row_of = token_ids // WW % WH
    col_of = token_ids % WW
    canon = ((level_of[:, None] * WZ + level_of[None, :]) * (WH * WH) + row_of[:, None] * WH + row_of[None, :]) * (2 * WW - 1)
    canon = canon + col_of[:, None] - col_of[None, :] + WW - 1
    return order[canon].astype(jnp.int32)


def shard_levels(rng, extent, pieces, low, top_value):
    factor_of, own = 1.0, jax.random.fold_in(rng, 6)
    for axis_at, shards_of in pieces:
        draws = jnp.exp(jax.random.uniform(jax.random.fold_in(own, axis_at), (shards_of,), jnp.float32, low / len(pieces), top_value / len(pieces)))
        factor_of = factor_of * jnp.repeat(draws, extent[axis_at] // shards_of).reshape([-1 if axis == axis_at else 1 for axis in range(len(extent))])
    return factor_of


def split_up(number_of, total, reach, skew):
    portions = [(1 << 20) // math.isqrt(rank ** skew) + 1 for rank in range(2, number_of + 1)]
    spare, holding = total - reach - (number_of - 1), [1] * (number_of - 1)
    while spare > 0:
        free = [i for i in range(number_of - 1) if holding[i] < reach]
        mass, left = sum([portions[i] for i in free]), spare
        for i in free:
            more = min(reach - holding[i], max(1, left * portions[i] // mass), spare)
            holding[i] = holding[i] + more
            spare = spare - more
    return np.array([reach] + holding)


def uneven(key, count, total, limit, skew):
    if count == 2:
        one = jax.random.randint(key, (), max(1, total - limit), min(limit, total - 1) + 1)
        return jnp.stack([one, total - one])
    tallies = jnp.asarray(split_up(count, total, limit, skew), jnp.int32)
    twos = (count - 1) // 2
    source_of, sink = tallies[1:1 + 2 * twos:2], tallies[2:2 + 2 * twos:2]
    room = jnp.minimum(source_of - 1, limit - sink)
    shifted = jax.random.randint(jax.random.fold_in(key, 1), (twos,), 0, 1 << 20) % (room + 1)
    tallies = tallies.at[1:1 + 2 * twos:2].set(source_of - shifted).at[2:2 + 2 * twos:2].set(sink + shifted)
    return tallies[jax.random.permutation(jax.random.fold_in(key, 2), count)]


def scatter_about(own_key, extent, deviation, bound, shards=(), dtype=jnp.bfloat16):
    gain = shard_levels(own_key, extent, shards, -0.22, 0.18) if shards else 1.0
    values = jax.random.normal(own_key, extent, jnp.float32) * deviation * gain
    return jnp.minimum(jnp.maximum(values, -bound), bound).astype(dtype)


def setup_inputs(seed: int = 0) -> dict:
    keys = jax.random.split(jax.random.key(seed), 12)
    return {
        "tokens": scatter_about(keys[0], (LEVELS, NLAT, NLON, C), 1.0, 6.0, ((1, 8), (2, 16))),
        "norm1_gain": jnp.clip(1.0 + 0.18 * jax.random.normal(keys[1], (C,), jnp.float32), 0.1, 1.9),
        "w_qkv": scatter_about(keys[2], (C, 3 * C), C ** -0.5, 0.4375),
        "w_proj": scatter_about(keys[3], (C, C), C ** -0.5, 0.4375),
        "bias_table": scatter_about(keys[4], (ZWIN, LATWIN, HEADS, POS), 1.0, 4.0, ((1, 8),), jnp.float32),
        "pos_index": draw_pos_index(jax.random.fold_in(keys[11], 71), 0),
        "mask_ids": jnp.searchsorted(jnp.cumsum(uneven(keys[6], NLAT // 6, NLAT, 12, 0)), jnp.arange(NLAT), side="right").astype(jnp.int32),
        "norm2_gain": jnp.clip(1.0 + 0.18 * jax.random.normal(keys[7], (C,), jnp.float32), 0.1, 1.9),
        "w_fc1": scatter_about(keys[8], (C, FFN), C ** -0.5, 0.4375),
        "w_fc2": scatter_about(keys[9], (FFN, C), FFN ** -0.5, 0.21875),
        "cotangent": scatter_about(keys[10], (LEVELS, NLAT, NLON, C), 1.0, 6.0, ((1, 8), (2, 16))),
    }


EPS = 1e-05
GELU_K = 0.7978845608
GELU_C = 0.044715

def norm_forward(field_in, norm_gain):
    center = field_in - lax.optimization_barrier(jnp.mean(field_in, axis=-1, keepdims=True))
    inv_std = lax.rsqrt(lax.optimization_barrier(jnp.mean(center * center, axis=-1, keepdims=True)) + EPS)
    normed = center * inv_std
    return (normed, inv_std, (normed * norm_gain).astype(jnp.bfloat16))

def norm_backward(d_output, normed, inv_std, norm_gain):
    d_norm = d_output * norm_gain
    mean_grad = lax.optimization_barrier(jnp.mean(d_norm, axis=-1, keepdims=True))
    mean_prod = lax.optimization_barrier(jnp.mean(d_norm * normed, axis=-1, keepdims=True))
    return inv_std * (d_norm - mean_grad - normed * mean_prod)

def mult(form, left, right):
    return jnp.einsum(form, left.astype(jnp.float32), right.astype(jnp.float32))

def window_split(field_in):
    levels, row_count, col_count, feature = field_in.shape
    win_part = field_in.reshape(levels // WZ, WZ, row_count // WH, WH, col_count // WW, WW, feature)
    win_part = win_part.transpose(0, 2, 4, 1, 3, 5, 6)
    return win_part.reshape(levels // WZ, row_count // WH, col_count // WW, WZ * WH * WW, feature)

def window_join(win_part):
    zone_w, row_w, col_w, win_size, feature = win_part.shape
    full_field = win_part.reshape(zone_w, row_w, col_w, WZ, WH, WW, feature).transpose(0, 3, 1, 4, 2, 5, 6)
    return full_field.reshape(zone_w * WZ, row_w * WH, col_w * WW, feature)

def window_allowed(mask_ids, levels):
    row_count = mask_ids.shape[0]
    top_flag = (jnp.arange(levels) == levels - 1).astype(jnp.int32)
    zone_ids = top_flag[:, None] + 2 * mask_ids[None, :]
    zone_ids = zone_ids.reshape(levels // WZ, WZ, row_count // WH, WH).transpose(0, 2, 1, 3)
    zone_ids = jnp.broadcast_to(zone_ids[..., None], zone_ids.shape + (WW,))
    zone_ids = zone_ids.reshape(levels // WZ, row_count // WH, WZ * WH * WW)
    return (zone_ids[..., :, None] == zone_ids[..., None, :]).astype(jnp.float32)

def attend_forward(windows, w_qkv, w_proj, bias, allowed):
    groups, win_count, win_size, feature = windows.shape
    head_count = bias.shape[1]
    head_dim = feature // head_count
    score_scale = head_dim ** (-0.5)
    proj_qkv = jnp.dot(windows.reshape(-1, feature), w_qkv, preferred_element_type=jnp.float32).astype(jnp.bfloat16)
    proj_qkv = proj_qkv.reshape(groups, win_count, win_size, 3, head_count, head_dim)
    queries = proj_qkv[:, :, :, 0]
    key_rows = proj_qkv[:, :, :, 1]
    values = proj_qkv[:, :, :, 2]
    scores = mult('gbqhd,gbkhd->gbhqk', queries, key_rows) * score_scale + bias[:, None]
    weighted = jnp.exp(scores) * allowed[:, None, None]
    attn_prob = weighted / lax.optimization_barrier(jnp.sum(weighted, axis=-1, keepdims=True))
    prob_low = attn_prob.astype(jnp.bfloat16)
    attended = mult('gbhqk,gbkhd->gbqhd', prob_low, values).astype(jnp.bfloat16).reshape(-1, feature)
    win_out = jnp.dot(attended, w_proj, preferred_element_type=jnp.float32).astype(jnp.bfloat16)
    return (win_out.reshape(windows.shape), (queries, key_rows, values, attn_prob, prob_low, attended))

def attend_backward(windows, w_qkv, w_proj, saved, d_output):
    queries, key_rows, values, attn_prob, prob_low, attended = saved
    groups, win_count, win_size, feature = windows.shape
    head_count = queries.shape[-2]
    head_dim = queries.shape[-1]
    score_scale = head_dim ** (-0.5)
    d_flat = d_output.reshape(-1, feature)
    grad_proj = jnp.dot(attended.T, d_flat, preferred_element_type=jnp.float32)
    d_att = jnp.dot(d_flat, w_proj.T, preferred_element_type=jnp.float32).astype(jnp.bfloat16)
    d_att = d_att.reshape(groups, win_count, win_size, head_count, head_dim)
    d_prob = mult('gbqhd,gbkhd->gbhqk', d_att, values)
    d_values = mult('gbhqk,gbqhd->gbkhd', prob_low, d_att).astype(jnp.bfloat16)
    d_scores = attn_prob * (d_prob - lax.optimization_barrier(jnp.sum(attn_prob * d_prob, axis=-1, keepdims=True)))
    d_low = (d_scores * score_scale).astype(jnp.bfloat16)
    d_queries = mult('gbhqk,gbkhd->gbqhd', d_low, key_rows).astype(jnp.bfloat16)
    d_keys = mult('gbhqk,gbqhd->gbkhd', d_low, queries).astype(jnp.bfloat16)
    d_qkv = jnp.stack([d_queries, d_keys, d_values], axis=3).reshape(-1, 3 * feature)
    grad_qkv = jnp.dot(windows.reshape(-1, feature).T, d_qkv, preferred_element_type=jnp.float32)
    d_windows = jnp.dot(d_qkv, w_qkv.T, preferred_element_type=jnp.float32).astype(jnp.bfloat16)
    return (d_windows.reshape(windows.shape), grad_qkv, grad_proj, lax.optimization_barrier(jnp.sum(d_scores, axis=1)))

def table_terms(d_bias, pos_index, entries):
    groups, head_count, win_size, _ = d_bias.shape
    flat_in = d_bias.reshape(groups * head_count, win_size * win_size).T
    summed = jax.ops.segment_sum(flat_in, pos_index.reshape(-1), num_segments=entries)
    return summed.T.reshape(groups, head_count, entries)

def mlp_pass(mid_field, cot_rows, norm_gain, w_fc1, w_fc2):
    normed, inv_std, hidden = norm_forward(mid_field, norm_gain)
    pre_act = jnp.dot(hidden, w_fc1, preferred_element_type=jnp.float32)
    inner = jnp.tanh(GELU_K * (pre_act + GELU_C * pre_act * pre_act * pre_act))
    act_low = (0.5 * pre_act * (1.0 + inner)).astype(jnp.bfloat16)
    block_rows = (mid_field + jnp.dot(act_low, w_fc2, preferred_element_type=jnp.float32)).astype(jnp.bfloat16)
    grad_fc2 = jnp.dot(act_low.T, cot_rows, preferred_element_type=jnp.float32)
    d_act = jnp.dot(cot_rows, w_fc2.T, preferred_element_type=jnp.float32)
    slope = 0.5 * (1.0 + inner) + 0.5 * pre_act * (1.0 - inner * inner) * GELU_K * (1.0 + 3.0 * GELU_C * pre_act * pre_act)
    d_pre = (d_act * slope).astype(jnp.bfloat16)
    grad_fc1 = jnp.dot(hidden.T, d_pre, preferred_element_type=jnp.float32)
    d_hidden = jnp.dot(d_pre, w_fc1.T, preferred_element_type=jnp.float32)
    grad_gain = lax.optimization_barrier(jnp.sum(d_hidden * normed, axis=0))
    d_mid = cot_rows.astype(jnp.float32) + norm_backward(d_hidden, normed, inv_std, norm_gain)
    return (block_rows, d_mid, grad_gain, grad_fc1, grad_fc2)

def reference(tokens, norm1_gain, w_qkv, w_proj, bias_table, pos_index, mask_ids, norm2_gain, w_fc1, w_fc2, cotangent):
    feature = tokens.shape[-1]
    field = tokens.astype(jnp.float32)
    normed1, inv_std1, hidden = norm_forward(field, norm1_gain)
    ahead = (-1, -(WH // 2), -(WW // 2))
    behind = (1, WH // 2, WW // 2)
    rolled = jnp.roll(hidden, ahead, axis=(0, 1, 2))
    by_rows = window_split(rolled).transpose(1, 0, 2, 3, 4)
    bias = jnp.take(bias_table, pos_index, axis=3).transpose(1, 0, 2, 3, 4)
    allowed = window_allowed(mask_ids, LEVELS).transpose(1, 0, 2, 3)

    def forward_row(items):
        win_rows, bias_rows, allow_rows = items
        win_out, saved = attend_forward(win_rows, w_qkv, w_proj, bias_rows, allow_rows)
        return win_out
    outs = lax.map(forward_row, (by_rows, bias, allowed))
    attn_field = jnp.roll(window_join(outs.transpose(1, 0, 2, 3, 4)), behind, axis=(0, 1, 2))
    mid_field = field + attn_field.astype(jnp.float32)

    def level_pass(items):
        mid_level, cot_level = items
        block_rows, d_mid, g_gain, g_fc1, g_fc2 = mlp_pass(mid_level.reshape(-1, feature), cot_level.reshape(-1, feature), norm2_gain, w_fc1, w_fc2)
        return (block_rows.reshape(mid_level.shape), d_mid.reshape(mid_level.shape), g_gain, g_fc1, g_fc2)
    block_out, d_mid, g_norm2, g_fc1, g_fc2 = lax.map(level_pass, (mid_field, cotangent))
    d_attn = jnp.roll(d_mid.astype(jnp.bfloat16), ahead, axis=(0, 1, 2))
    d_rows = window_split(d_attn).transpose(1, 0, 2, 3, 4)

    def backward_row(carry, items):
        win_rows, bias_rows, allow_rows, d_out_rows = items
        win_out, saved = attend_forward(win_rows, w_qkv, w_proj, bias_rows, allow_rows)
        d_win, g_qkv, g_proj, d_bias = attend_backward(win_rows, w_qkv, w_proj, saved, d_out_rows)
        return ((carry[0] + g_qkv, carry[1] + g_proj), (d_win, table_terms(d_bias, pos_index, POS)))
    start = (jnp.zeros((feature, 3 * feature), jnp.float32), jnp.zeros((feature, feature), jnp.float32))
    (g_qkv, g_proj), (d_win, g_table) = lax.scan(backward_row, start, (by_rows, bias, allowed, d_rows))
    d_hidden = jnp.roll(window_join(d_win.transpose(1, 0, 2, 3, 4)), behind, axis=(0, 1, 2)).astype(jnp.float32)
    g_norm1 = lax.optimization_barrier(jnp.sum(d_hidden * normed1, axis=(0, 1, 2)))
    grad_tokens = (d_mid + norm_backward(d_hidden, normed1, inv_std1, norm1_gain)).astype(jnp.bfloat16)
    factor = float(TOKENS) ** (-0.5)
    grad_table = g_table.transpose(1, 0, 2, 3) * factor
    return (block_out, grad_tokens, g_norm1 * factor, g_qkv * factor, g_proj * factor, grad_table, lax.optimization_barrier(jnp.sum(g_norm2, axis=0)) * factor, lax.optimization_barrier(jnp.sum(g_fc1, axis=0)) * factor, lax.optimization_barrier(jnp.sum(g_fc2, axis=0)) * factor)
```

```python
import jax
import jax.numpy as jnp
from jax import lax
from jax.experimental import pallas as pl
from jax.experimental.pallas import tpu as pltpu
from jax.sharding import PartitionSpec as P

F32 = jnp.float32
BF16 = jnp.bfloat16
C = 192
HEADS = 6
FFN = 768
WIN = 144
NWIN = 8
TOK = 1152
POS = 3312
EPS = 1e-05
GELU_K = 0.7978845608
GELU_C = 0.044715
LOG2E = 1.4426950408889634
LN2 = 0.6931471805599453
SCALE = 32 ** -0.5
FACTOR = 147456.0 ** -0.5


def nn(a, b):
    return lax.dot_general(a, b, (((1,), (0,)), ((), ())), preferred_element_type=F32)


def nt(a, b):
    return lax.dot_general(a, b, (((1,), (1,)), ((), ())), preferred_element_type=F32)


def tn(a, b):
    return lax.dot_general(a, b, (((0,), (0,)), ((), ())), preferred_element_type=F32)


def head_mask(h, dtype):
    lane = lax.broadcasted_iota(jnp.int32, (1, C), 1)
    inside = (lane >= h * 32) & (lane < h * 32 + 32)
    return jnp.where(inside, 1.0, 0.0).astype(dtype)


def spread_heads(x):
    return jnp.concatenate([x * head_mask(h, BF16) for h in range(HEADS)], axis=0)


def pick_heads(x):
    total = x[:WIN] * head_mask(0, F32)
    for h in range(1, HEADS):
        total = total + x[h * WIN : (h + 1) * WIN] * head_mask(h, F32)
    return total


def mean_of(x):
    return jnp.sum(x, axis=-1, keepdims=True) * (1.0 / C)


def norm_stats(x):
    center = x - mean_of(x)
    inv = lax.rsqrt(mean_of(center * center) + EPS)
    return center * inv, inv


def norm_back(g, normed, inv):
    return inv * (g - mean_of(g) - normed * mean_of(g * normed))


def prep_bias(table_ref, idx_ref, mask_ref, bias_ref):
    sub = lax.broadcasted_iota(jnp.int32, (16, 256), 0)
    lane = lax.broadcasted_iota(jnp.int32, (16, 256), 1)
    lane_row = lane // 12
    col = lane - lane_row * 12
    top_i = jnp.where(sub >= 6, 1, 0)
    top_j = jnp.where(lane_row >= 6, 1, 0)
    row_i = sub - 6 * top_i
    row_j = lane_row - 6 * top_j
    zone_i = jnp.zeros((16, 256), jnp.int32)
    zone_j = jnp.zeros((16, 256), jnp.int32)
    for r in range(6):
        zone_i = jnp.where(row_i == r, 2 * mask_ref[r], zone_i)
        zone_j = jnp.where(row_j == r, 2 * mask_ref[r], zone_j)
    idx = idx_ref[...]
    hi = idx >> 7
    lo = idx & 127

    def one(zh, carry):
        row = table_ref[zh] * LOG2E
        tiles = []
        for t in range(2):
            lo_t = lo[:, t * 128 : (t + 1) * 128]
            hi_t = hi[:, t * 128 : (t + 1) * 128]
            acc = jnp.zeros((32, 128), F32)
            for a in range(26):
                part = row[:, a * 128 : min(POS, (a + 1) * 128)]
                if a == 25:
                    part = jnp.concatenate([part, jnp.zeros((1, 16), F32)], axis=1)
                got = jnp.take_along_axis(jnp.broadcast_to(part, (32, 128)), lo_t, axis=1)
                acc = jnp.where(hi_t == a, got, acc)
            tiles.append(acc)
        both = jnp.concatenate(tiles, axis=1)
        upper, lower = both[:16], both[16:]
        flag = jnp.where(zh >= HEADS, 1, 0)
        same = (zone_i + top_i * flag) == (zone_j + top_j * flag)
        mask = jnp.where(same, 0.0, -1e30)
        for c in range(12):
            ahead = pltpu.roll(upper, c, 1) if c else upper
            val = jnp.where(col >= c, ahead, pltpu.roll(lower, 256 - 12 + c, 1)) + mask
            bias_ref[0, zh, pl.ds(c, 12, stride=12), :] = val[:12, :128]
            bias_ref[1, zh, pl.ds(c, 12, stride=12), :] = val[:12, 128:]
        return carry

    lax.fori_loop(0, 12, one, 0)


def assemble(ext_ref, win_ref):
    for level in range(4):
        for r in range(6):
            slab = ext_ref[(level + 1) % 4, r, :, :].astype(F32)
            for w in range(4):
                start = ((level // 2) * 4 + w) * WIN + ((level % 2) * 6 + r) * 12
                win_ref[start : start + 12, :] = slab[6 + 12 * w : 18 + 12 * w]


def disassemble(win_ref, slab_ref, ext_ref):
    for level in range(4):
        for r in range(6):
            k = r % 2
            for w in range(4):
                start = ((level // 2) * 4 + w) * WIN + ((level % 2) * 6 + r) * 12
                slab_ref[k, 6 + 12 * w : 18 + 12 * w, :] = win_ref[start : start + 12, :]
            ext_ref[(level + 1) % 4, r, :, :] = slab_ref[k].astype(BF16)


def forward_window(wi, s):
    rows = pl.ds(pl.multiple_of(wi * WIN, WIN), WIN)
    z = wi // 4
    x = s.x[rows, :]
    normed1, inv1 = norm_stats(x)
    hid = (normed1 * s.n1[...]).astype(BF16)
    s.normed1[rows, :] = normed1
    s.inv1[rows, :] = inv1
    s.hid[rows, :] = hid
    q = (nn(hid, s.wq[0]) * (SCALE * LOG2E)).astype(BF16)
    k = nn(hid, s.wq[1]).astype(BF16)
    v = nn(hid, s.wq[2]).astype(BF16)
    s.k[rows, :] = k
    s.v[rows, :] = v
    qm = spread_heads(q)
    s.q[rows, :] = q
    scores = nt(qm, k)
    b0 = s.bias[0, pl.ds(z * 6, 6)].reshape(864, 128)
    b1 = s.bias[1, pl.ds(z * 6, 6)].reshape(864, 128)
    bias = jnp.concatenate([b0, b1], axis=1)[:, :WIN]
    e = jnp.exp2(scores + bias)
    p = (e * (1.0 / jnp.sum(e, axis=-1, keepdims=True))).astype(BF16)
    s.p[wi] = p
    att = pick_heads(nn(p, v)).astype(BF16)
    s.att[rows, :] = att
    mid = x + nn(att, s.wp[...]).astype(BF16).astype(F32)
    normed2, inv2 = norm_stats(mid)
    hid2 = (normed2 * s.n2[...]).astype(BF16)
    s.hid2[rows, :] = hid2
    pre = nn(hid2, s.w1[...])
    u = pre * pre
    t = jnp.tanh(pre * (GELU_K + (GELU_K * GELU_C) * u))
    half = 0.5 + 0.5 * t
    act = pre * half
    slope = half + act * (1.0 - half) * (2.0 * GELU_K + (6.0 * GELU_K * GELU_C) * u)
    act = act.astype(BF16)
    s.act[rows, :] = act
    s.blk[rows, :] = mid + nt(act, s.w2[...])
    cot = s.cot[rows, :]
    d_act = nn(cot.astype(BF16), s.w2[...])
    d_pre = (d_act * slope).astype(BF16)
    s.d_pre[rows, :] = d_pre
    d_hid2 = nt(d_pre, s.w1[...])
    s.gn[1:2, :] += jnp.sum(d_hid2 * normed2, axis=0, keepdims=True)
    s.d_mid[rows, :] = cot + norm_back(d_hid2 * s.n2[...], normed2, inv2)


def backward_window(wi, s):
    rows = pl.ds(pl.multiple_of(wi * WIN, WIN), WIN)
    z = wi // 4
    d_mid = s.d_mid[rows, :]
    d_att = nt(d_mid.astype(BF16), s.wp[...]).astype(BF16)
    dom = spread_heads(d_att)
    v = s.v[rows, :]
    p = s.p[wi]
    d_p = nt(dom, v)
    d_v = tn(p, dom).astype(BF16)
    pf = p.astype(F32)
    pd = pf * d_p
    d_s = pd - pf * jnp.sum(pd, axis=-1, keepdims=True)
    s.d_bias[0, pl.ds(z * 6, 6)] += d_s[:, :128].reshape(6, WIN, 128)
    s.d_bias[1, pl.ds(z * 6, 6), :, 0:16] += d_s[:, 128:].reshape(6, WIN, 16)
    d_low = d_s.astype(BF16)
    d_k = (tn(d_low, spread_heads(s.q[rows, :])) * LN2).astype(BF16)
    d_q = (pick_heads(nn(d_low, s.k[rows, :])) * SCALE).astype(BF16)
    s.dq[rows, :] = d_q
    s.dk[rows, :] = d_k
    s.dv[rows, :] = d_v
    d_win = nt(d_q, s.wq[0]) + nt(d_k, s.wq[1]) + nt(d_v, s.wq[2])
    d_hid = d_win.astype(BF16).astype(F32)
    normed1 = s.normed1[rows, :]
    s.gn[0:1, :] += jnp.sum(d_hid * normed1, axis=0, keepdims=True)
    s.x[rows, :] = d_mid + norm_back(d_hid * s.n1[...], normed1, s.inv1[rows, :])


def table_back(idx_ref, d_bias_ref, can_ref, lhs_ref, out_ref):
    lane = lax.broadcasted_iota(jnp.int32, (12, 256), 1)
    col = lane - (lane // 12) * 12

    def one(zh, carry):
        up = jnp.zeros((12, 256), F32)
        down = jnp.zeros((12, 256), F32)
        for c in range(12):
            x0 = d_bias_ref[0, zh, pl.ds(c, 12, stride=12), :]
            x1 = d_bias_ref[1, zh, pl.ds(c, 12, stride=12), :]
            x = jnp.concatenate([x0, x1], axis=1)
            over = jnp.where(col >= c, x, 0.0)
            up = up + (pltpu.roll(over, 256 - c, 1) if c else over)
            if c:
                down = down + pltpu.roll(x - over, 12 - c, 1)
        can_ref[0, zh, 0:12, :] = up
        can_ref[1, zh, 0:12, :] = down
        return carry

    lax.fori_loop(0, 12, one, 0)
    acc = jnp.zeros((26 * 16, 128), F32)
    entry = lax.broadcasted_iota(jnp.int32, (128, 256), 0)
    for part in range(2):
        for lr in range(12):
            idx = idx_ref[part * 16 + lr : part * 16 + lr + 1, :]
            ok = lax.broadcasted_iota(jnp.int32, (1, 256), 1) < WIN
            if part == 1:
                spot = lax.broadcasted_iota(jnp.int32, (1, 256), 1)
                ok = ok & (spot - (spot // 12) * 12 > 0)
            hi = jnp.where(ok, idx >> 7, 99)
            lo = idx & 127
            here = jnp.where(entry == lo, 1.0, 0.0).astype(BF16)
            d = can_ref[part, :, lr, :]
            for a in range(26):
                lhs_ref[a * 16 : (a + 1) * 16, :] = jnp.where(hi == a, d, 0.0).astype(BF16)
            acc = acc + nt(lhs_ref[...], here)
    out_ref[...] = acc


class Refs:
    pass


NAMES = [
    ("wq", (3, C, C), BF16),
    ("bias", (2, 12, WIN, 128), F32),
    ("d_bias", (2, 12, WIN, 128), F32),
    ("x", (TOK, C), F32),
    ("cot", (TOK, C), F32),
    ("blk", (TOK, C), F32),
    ("d_mid", (TOK, C), F32),
    ("normed1", (TOK, C), F32),
    ("inv1", (TOK, 1), F32),
    ("hid", (TOK, C), BF16),
    ("q", (TOK, C), BF16),
    ("k", (TOK, C), BF16),
    ("v", (TOK, C), BF16),
    ("p", (NWIN, 864, WIN), BF16),
    ("att", (TOK, C), BF16),
    ("hid2", (TOK, C), BF16),
    ("act", (TOK, FFN), BF16),
    ("d_pre", (TOK, FFN), BF16),
    ("dq", (TOK, C), BF16),
    ("dk", (TOK, C), BF16),
    ("dv", (TOK, C), BF16),
    ("gn", (8, C), F32),
    ("gall", (C, FFN), F32),
    ("can", (2, 16, 16, 256), F32),
    ("lhs", (26 * 16, 256), BF16),
    ("tab", (26 * 16, 128), F32),
    ("slab", (2, 64, C), F32),
    ("tab2", (320, 128), F32),
    ("norms", (16, 128), F32),
    ("ext_tok", (4, 6, 64, C), BF16),
    ("ext_cot", (4, 6, 64, C), BF16),
    ("e_blk", (4, 6, 64, C), BF16),
    ("e_tok", (4, 6, 64, C), BF16),
    ("f_own", (2 * C, FFN), BF16),
    ("f_lon", (16, 48, 384), BF16),
    ("f_lat", (8, 48, 384), BF16),
    ("f_fin", (48, 384), BF16),
    ("t_own", (16, 96, 128), BF16),
    ("t_lon", (16, 96, 128), BF16),
    ("t_lat", (8, 96, 128), BF16),
    ("t_fin", (96, 128), BF16),
]


def pack_table(s):
    t_out = s.t_own
    for a in range(26):
        s.tab2[a * 12 : (a + 1) * 12, :] = s.tab[a * 16 : a * 16 + 12, :]
    for p in range(12, 16):
        t_out[p, 0:80, :] = s.tab2[(p - 12) * 80 : (p - 11) * 80, :].astype(BF16)
        t_out[p, 80:96, :] = jnp.zeros((16, 128), BF16)
    t_out[12, 80:96, :] = s.norms[...].astype(BF16)


SEMS = [
    ("local", 10),
    ("in_send", 6),
    ("in_recv", 6),
    ("out_send", 6),
    ("out_recv", 6),
    ("fa_send", 16),
    ("fa_recv", 16),
    ("fb_send", 8),
    ("fb_recv", 8),
    ("fc_send", 16),
    ("fc_recv", 16),
    ("ta_send", 16),
    ("ta_recv", 16),
    ("tb_send", 8),
    ("tb_recv", 8),
    ("tc_send", 16),
    ("tc_recv", 16),
]


def remote(src, dst, send, recv, where):
    return pltpu.make_async_remote_copy(
        src_ref=src, dst_ref=dst, send_sem=send, recv_sem=recv, device_id=where, device_id_type=pl.DeviceIdType.MESH
    )


def each_peer(count, me, start, stop, body):
    def one(p, carry):
        @pl.when(p != me)
        def _():
            body(p)

        return carry

    lax.fori_loop(start, stop, one, 0)


def main_kernel(
    tok, cot, n1, wqkv, wp, table, idx, mask, n2, w1, w2,
    blk_main, blk_cols, gtok_main, gtok_cols, f_res, t_res, *scratch
):
    s = Refs()
    for (name, _, _), ref in zip(NAMES, scratch):
        setattr(s, name, ref)
    for (name, _), ref in zip(SEMS, scratch[len(NAMES) :]):
        setattr(s, name, ref)
    s.n1, s.n2, s.wp, s.w1, s.w2 = n1, n2, wp, w1, w2
    lon = lax.axis_index("lon")
    lat = lax.axis_index("lat")
    lon_up, lon_down = lax.rem(lon + 1, 16), lax.rem(lon + 15, 16)
    lat_up, lat_down = lax.rem(lat + 1, 8), lax.rem(lat + 7, 8)
    barrier = pltpu.get_barrier_semaphore()

    def greet(a, b):
        pl.semaphore_signal(
            barrier, inc=1, device_id={"lon": a, "lat": b}, device_id_type=pl.DeviceIdType.MESH
        )

    each_peer(16, lon, 0, 16, lambda p: greet(p, lat))
    each_peer(8, lat, 0, 8, lambda p: greet(lon, p))
    greet(lon_up, lat_up)
    greet(lon_down, lat_down)

    locals_in = []
    for i, (src, dst) in enumerate(((tok, s.ext_tok), (cot, s.ext_cot))):
        copy = pltpu.make_async_copy(src.at[:, 3:6], dst.at[:, 0:3, 0:48], s.local.at[i])
        copy.start()
        locals_in.append(copy)
    pl.semaphore_wait(barrier, 24)
    halo_in = []
    for i, (src, dst) in enumerate(((tok, s.ext_tok), (cot, s.ext_cot))):
        moves = (
            (src.at[:, 0:3], dst.at[:, 3:6, 0:48], {"lon": lon, "lat": lat_down}),
            (src.at[:, 3:6, 0:16], dst.at[:, 0:3, 48:64], {"lon": lon_down, "lat": lat}),
            (src.at[:, 0:3, 0:16], dst.at[:, 3:6, 48:64], {"lon": lon_down, "lat": lat_down}),
        )
        for k, (a, b, where) in enumerate(moves):
            copy = remote(a, b, s.in_send.at[3 * i + k], s.in_recv.at[3 * i + k], where)
            copy.start()
            halo_in.append(copy)

    for i in range(3):
        s.wq[i] = wqkv[:, i * C : (i + 1) * C]
    for ref in (s.d_bias, s.gn, s.can, s.slab, s.tab2, s.norms):
        ref[...] = jnp.zeros_like(ref)
    prep_bias(table, idx, mask, s.bias)
    locals_in[0].wait()
    for copy in halo_in[:3]:
        copy.wait_recv()
    assemble(s.ext_tok, s.x)
    locals_in[1].wait()
    for copy in halo_in[3:]:
        copy.wait_recv()
    assemble(s.ext_cot, s.cot)
    for copy in halo_in:
        copy.wait_send()

    def window_loop(body, start, stop):
        lax.fori_loop(start, stop, lambda i, c: (body(i, s), c)[1], 0)

    def send_out(i, e, main, cols):
        copy = pltpu.make_async_copy(e.at[:, 0:3, 0:48], main.at[:, 3:6], s.local.at[2 + i])
        copy.start()
        copies = [copy]
        moves = (
            (e.at[:, 3:6, 0:48], main.at[:, 0:3], {"lon": lon, "lat": lat_up}),
            (e.at[:, 0:3, 48:64], cols.at[:, 3:6], {"lon": lon_up, "lat": lat}),
            (e.at[:, 3:6, 48:64], cols.at[:, 0:3], {"lon": lon_up, "lat": lat_up}),
        )
        for k, (a, b, where) in enumerate(moves):
            copy = remote(a, b, s.out_send.at[3 * i + k], s.out_recv.at[3 * i + k], where)
            copy.start()
            copies.append(copy)
        return copies

    def lon_scatter(piece, slots, send, recv, start, stop):
        def go(p):
            remote(piece(p), slots.at[lon], send.at[p], recv.at[lon], {"lon": p, "lat": lat}).start()

        each_peer(16, lon, start, stop, go)

    def lon_scatter_wait(piece, slots, send, recv):
        def done(p):
            copy = remote(piece(p), slots.at[p], send.at[p], recv.at[p], {"lon": p, "lat": lat})
            copy.wait_send()
            copy.wait_recv()

        each_peer(16, lon, 0, 16, done)

    def lat_spread(slots, send, recv):
        def go(p):
            remote(slots.at[lat], slots.at[lat], send.at[p], recv.at[lat], {"lon": lon, "lat": p}).start()

        each_peer(8, lat, 0, 8, go)

    def lat_spread_wait(slots, send, recv):
        def done(p):
            copy = remote(slots.at[lat], slots.at[p], send.at[p], recv.at[p], {"lon": lon, "lat": p})
            copy.wait_send()
            copy.wait_recv()

        each_peer(8, lat, 0, 8, done)

    def lon_spread(src, slots, local, send, recv):
        pltpu.make_async_copy(src, slots.at[lon], local).start()

        def go(p):
            remote(src, slots.at[lon], send.at[p], recv.at[lon], {"lon": p, "lat": lat}).start()

        each_peer(16, lon, 0, 16, go)

    def lon_spread_wait(src, slots, local, send, recv):
        pltpu.make_async_copy(src, slots.at[lon], local).wait()

        def done(p):
            copy = remote(src, slots.at[p], send.at[p], recv.at[p], {"lon": p, "lat": lat})
            copy.wait_send()
            copy.wait_recv()

        each_peer(16, lon, 0, 16, done)

    def f_piece(p):
        g = p // 2
        half = p - 2 * g
        return s.f_own.at[pl.ds(pl.multiple_of(g * 48, 48), 48), pl.ds(pl.multiple_of(half * 384, 384), 384)]

    def t_piece(p):
        return s.t_own.at[p]

    def total(slots, count):
        acc = slots[0].astype(F32)
        for i in range(1, count):
            acc = acc + slots[i].astype(F32)
        return acc

    window_loop(forward_window, 0, NWIN)
    s.f_own[0:C, :] = tn(s.hid2[...], s.d_pre[...]).astype(BF16)
    s.f_own[C : 2 * C, :] = tn(s.cot[...].astype(BF16), s.act[...]).astype(BF16)
    lon_scatter(f_piece, s.f_lon, s.fa_send, s.fa_recv, 0, 16)
    s.f_lon[lon] = f_piece(lon)[...]
    disassemble(s.blk, s.slab, s.e_blk)
    out_copies = send_out(0, s.e_blk, blk_main, blk_cols)

    window_loop(backward_window, 0, 3)
    lon_scatter_wait(f_piece, s.f_lon, s.fa_send, s.fa_recv)
    s.f_lat[lat] = total(s.f_lon, 16).astype(BF16)
    lat_spread(s.f_lat, s.fb_send, s.fb_recv)
    window_loop(backward_window, 3, 5)
    lat_spread_wait(s.f_lat, s.fb_send, s.fb_recv)
    s.f_fin[...] = total(s.f_lat, 8).astype(BF16)
    lon_spread(s.f_fin, f_res, s.local.at[4], s.fc_send, s.fc_recv)
    window_loop(backward_window, 5, NWIN)

    hid = s.hid[...]
    s.gall[:, 0:C] = tn(hid, s.dq[...])
    s.gall[:, C : 2 * C] = tn(hid, s.dk[...])
    s.gall[:, 2 * C : 3 * C] = tn(hid, s.dv[...])
    s.gall[:, 3 * C : 4 * C] = tn(s.att[...], s.d_mid[...].astype(BF16))
    for p in range(12):
        for t in range(6):
            part = s.gall[p * 16 : (p + 1) * 16, t * 128 : (t + 1) * 128]
            s.t_own[p, t * 16 : (t + 1) * 16, :] = part.astype(BF16)
    lon_scatter(t_piece, s.t_lon, s.ta_send, s.ta_recv, 0, 12)
    disassemble(s.x, s.slab, s.e_tok)
    out_copies += send_out(1, s.e_tok, gtok_main, gtok_cols)
    table_back(idx, s.d_bias, s.can, s.lhs, s.tab)
    for i in range(2):
        s.norms[2 * i : 2 * i + 1, :] = s.gn[i : i + 1, 0:128]
        s.norms[2 * i + 1 : 2 * i + 2, 0:64] = s.gn[i : i + 1, 128:C]
    pack_table(s)
    lon_scatter(t_piece, s.t_lon, s.ta_send, s.ta_recv, 12, 16)
    s.t_lon[lon] = s.t_own[lon]
    lon_scatter_wait(t_piece, s.t_lon, s.ta_send, s.ta_recv)
    s.t_lat[lat] = total(s.t_lon, 16).astype(BF16)
    lat_spread(s.t_lat, s.tb_send, s.tb_recv)
    lat_spread_wait(s.t_lat, s.tb_send, s.tb_recv)
    sub = lax.broadcasted_iota(jnp.int32, (96, 128), 0)
    keep = (sub < 80) & (jnp.zeros((96, 128), jnp.int32) + lon >= 12)
    s.t_fin[...] = jnp.where(keep, s.t_lat[lat].astype(F32), total(s.t_lat, 8)).astype(BF16)
    lon_spread(s.t_fin, t_res, s.local.at[5], s.tc_send, s.tc_recv)
    lon_spread_wait(s.f_fin, f_res, s.local.at[4], s.fc_send, s.fc_recv)
    out_copies[0].wait()
    out_copies[4].wait()
    for copy in out_copies[1:4] + out_copies[5:]:
        copy.wait_send()
        copy.wait_recv()
    lon_spread_wait(s.t_fin, t_res, s.local.at[5], s.tc_send, s.tc_recv)


def finish_kernel(
    blk_main, blk_cols, gtok_main, gtok_cols, f_res, t_res,
    block, gtok, gn1, gqkv, gproj, gtable, gn2, gfc1, gfc2, w_full, tab2
):
    col = lax.broadcasted_iota(jnp.int32, (16, C), 0)
    for main, cols, out in ((blk_main, blk_cols, block), (gtok_main, gtok_cols, gtok)):
        for level in range(4):
            for r in range(6):
                edge = jnp.where(col < 6, cols[level, r].astype(F32), main[level, r, 0:16, :].astype(F32))
                out[level, r, 0:16, :] = edge.astype(BF16)
                out[level, r, 16:48, :] = main[level, r, 16:48, :]
    for p in range(16):
        out = gfc1 if p < 8 else gfc2
        g, half = (p // 2) % 4, p % 2
        out[g * 48 : (g + 1) * 48, half * 384 : (half + 1) * 384] = f_res[p].astype(F32) * FACTOR
    for p in range(12):
        for t in range(6):
            part = t_res[p, t * 16 : (t + 1) * 16, :].astype(F32) * FACTOR
            w_full[p * 16 : (p + 1) * 16, t * 128 : (t + 1) * 128] = part
    gqkv[...] = w_full[:, 0:576]
    gproj[...] = w_full[:, 576:768]
    for p in range(12, 16):
        tab2[(p - 12) * 80 : (p - 11) * 80, :] = t_res[p, 0:80, :].astype(F32) * FACTOR
    for a in range(26):
        width = min(128, POS - a * 128)
        for k in range(12):
            gtable[k, :, a * 128 : a * 128 + width] = tab2[a * 12 + k : a * 12 + k + 1, 0:width]
    norms = t_res[12, 80:96, :].astype(F32) * FACTOR
    for i, out in enumerate((gn1, gn2)):
        out[:, 0:128] = norms[2 * i : 2 * i + 1, :]
        out[:, 128:C] = norms[2 * i + 1 : 2 * i + 2, 0:64]


def index_tables(pos_index):
    up = pos_index[::12, :]
    down = pos_index[:, ::12].reshape(12, 12, 12)
    down = jnp.concatenate([down[:, :1], down[:, :0:-1]], axis=1).transpose(0, 2, 1).reshape(12, WIN)
    both = jnp.stack([up, down])
    return jnp.pad(both, ((0, 0), (0, 4), (0, 112))).reshape(32, 256)


def shards(tokens, norm1_gain, w_qkv, w_proj, bias_table, pos_index, mask_ids, norm2_gain, w_fc1, w_fc2, cotangent):
    vm = pl.BlockSpec(memory_space=pltpu.VMEM)
    anywhere = pl.BlockSpec(memory_space=pl.ANY)
    main = jax.ShapeDtypeStruct((4, 6, 48, C), BF16)
    cols = jax.ShapeDtypeStruct((4, 6, 16, C), BF16)
    outs = pl.pallas_call(
        main_kernel,
        out_shape=[
            main, cols, main, cols,
            jax.ShapeDtypeStruct((16, 48, 384), BF16),
            jax.ShapeDtypeStruct((16, 96, 128), BF16),
        ],
        in_specs=[anywhere] * 2 + [vm] * 5 + [pl.BlockSpec(memory_space=pltpu.SMEM)] + [vm] * 3,
        out_specs=[anywhere] * 6,
        scratch_shapes=[pltpu.VMEM(shape, dtype) for _, shape, dtype in NAMES]
        + [pltpu.SemaphoreType.DMA((n,)) for _, n in SEMS],
        compiler_params=pltpu.CompilerParams(
            vmem_limit_bytes=56 * 1024 * 1024, collective_id=0, has_side_effects=True
        ),
    )(
        tokens, cotangent, norm1_gain.reshape(1, C), w_qkv, w_proj,
        bias_table.transpose(0, 2, 1, 3).reshape(12, 1, POS), index_tables(pos_index), mask_ids,
        norm2_gain.reshape(1, C), w_fc1, w_fc2.T,
    )
    f32 = lambda *shape: jax.ShapeDtypeStruct(shape, F32)
    block, gtok, gn1, gqkv, gproj, gtable, gn2, gfc1, gfc2 = pl.pallas_call(
        finish_kernel,
        out_shape=[main, main, f32(1, C), f32(C, 576), f32(C, C), f32(12, 1, POS), f32(1, C), f32(C, FFN), f32(C, FFN)],
        in_specs=[vm] * 6,
        out_specs=[vm] * 9,
        scratch_shapes=[pltpu.VMEM((C, FFN), F32), pltpu.VMEM((320, 128), F32)],
        compiler_params=pltpu.CompilerParams(vmem_limit_bytes=40 * 1024 * 1024),
    )(*outs)
    gtable = gtable.reshape(2, 6, 1, POS).transpose(0, 2, 1, 3)
    return (block, gtok, gn1.reshape(C), gqkv, gproj, gtable, gn2.reshape(C), gfc1, gfc2.T)


def solution(mesh):
    act = P(None, "lat", "lon", None)
    table = P(None, "lat", None, None)
    return jax.shard_map(
        shards,
        mesh=mesh,
        in_specs=(act, P(), P(), P(), table, P(), P("lat"), P(), P(), P(), act),
        out_specs=(act, act, P(), P(), P(), table, P(), P(), P()),
        check_vma=False,
    )
```

```python
import jax
import jax.numpy as jnp
from jax import lax
from jax.experimental import pallas as pl
from jax.experimental.pallas import tpu as pltpu
from jax.sharding import PartitionSpec as P

F32 = jnp.float32
BF16 = jnp.bfloat16
C = 192
HEADS = 6
FFN = 768
WIN = 144
NWIN = 8
TOK = 1152
POS = 3312
EPS = 1e-05
GELU_K = 0.7978845608
GELU_C = 0.044715
LOG2E = 1.4426950408889634
LN2 = 0.6931471805599453
SCALE = 32 ** -0.5
FACTOR = 147456.0 ** -0.5


def nn(a, b):
    return lax.dot_general(a, b, (((1,), (0,)), ((), ())), preferred_element_type=F32)


def nt(a, b):
    return lax.dot_general(a, b, (((1,), (1,)), ((), ())), preferred_element_type=F32)


def tn(a, b):
    return lax.dot_general(a, b, (((0,), (0,)), ((), ())), preferred_element_type=F32)


def head_mask(h, dtype):
    lane = lax.broadcasted_iota(jnp.int32, (1, C), 1)
    inside = (lane >= h * 32) & (lane < h * 32 + 32)
    return jnp.where(inside, 1.0, 0.0).astype(dtype)


def spread_heads(x):
    return jnp.concatenate([x * head_mask(h, BF16) for h in range(HEADS)], axis=0)


def pick_heads(x):
    total = x[:WIN] * head_mask(0, F32)
    for h in range(1, HEADS):
        total = total + x[h * WIN : (h + 1) * WIN] * head_mask(h, F32)
    return total


def mean_of(x):
    return jnp.sum(x, axis=-1, keepdims=True) * (1.0 / C)


def norm_stats(x):
    center = x - mean_of(x)
    inv = lax.rsqrt(mean_of(center * center) + EPS)
    return center * inv, inv


def norm_back(g, normed, inv):
    return inv * (g - mean_of(g) - normed * mean_of(g * normed))


def zone_row(mask_ref, out_ref):
    lane = lax.broadcasted_iota(jnp.int32, (8, 128), 1)
    ids = jnp.zeros((8, 128), jnp.int32)
    for r in range(6):
        ids = jnp.where(lane == r, 2 * mask_ref[r], ids)
    out_ref[...] = ids.astype(F32)


def prep_bias(z, table_ref, idx_ref, zone_ref, bias_ref):
    sub = lax.broadcasted_iota(jnp.int32, (16, 256), 0)
    lane = lax.broadcasted_iota(jnp.int32, (16, 256), 1)
    lane_row = lane // 12
    col = lane - lane_row * 12
    top_i = jnp.where(sub >= 6, 1, 0)
    top_j = jnp.where(lane_row >= 6, 1, 0)
    row_i = sub - 6 * top_i
    row_j = lane_row - 6 * top_j
    zone_i = top_i.astype(F32) if z == 1 else jnp.zeros((16, 256), F32)
    zone_j = top_j.astype(F32) if z == 1 else jnp.zeros((16, 256), F32)
    for r in range(6):
        here = jnp.broadcast_to(zone_ref[0:1, r : r + 1], (16, 256))
        zone_i = zone_i + jnp.where(row_i == r, here, 0.0)
        zone_j = zone_j + jnp.where(row_j == r, here, 0.0)
    mask = jnp.where(zone_i == zone_j, 0.0, -1e30)
    idx = idx_ref[...]
    hi = idx >> 7
    lo = idx & 127

    def one(h, carry):
        row = table_ref[h] * LOG2E
        tiles = []
        for t in range(2):
            lo_t = lo[:, t * 128 : (t + 1) * 128]
            hi_t = hi[:, t * 128 : (t + 1) * 128]
            acc = jnp.zeros((32, 128), F32)
            for a in range(26):
                part = row[:, a * 128 : min(POS, (a + 1) * 128)]
                if a == 25:
                    part = jnp.concatenate([part, jnp.zeros((1, 16), F32)], axis=1)
                got = jnp.take_along_axis(jnp.broadcast_to(part, (32, 128)), lo_t, axis=1)
                acc = jnp.where(hi_t == a, got, acc)
            tiles.append(acc)
        both = jnp.concatenate(tiles, axis=1)
        upper, lower = both[:16], both[16:]
        for c in range(12):
            ahead = pltpu.roll(upper, c, 1) if c else upper
            val = jnp.where(col >= c, ahead, pltpu.roll(lower, 256 - 12 + c, 1)) + mask
            bias_ref[0, 6 * z + h, pl.ds(c, 12, stride=12), :] = val[:12, :128]
            bias_ref[1, 6 * z + h, pl.ds(c, 12, stride=12), :] = val[:12, 128:]
        return carry

    lax.fori_loop(0, 6, one, 0)


def assemble(ext_ref, win_ref, z):
    for level in (2 * z, 2 * z + 1):
        for r in range(6):
            slab = ext_ref[(level + 1) % 4, r, :, :].astype(F32)
            for w in range(4):
                start = (z * 4 + w) * WIN + ((level % 2) * 6 + r) * 12
                win_ref[start : start + 12, :] = slab[6 + 12 * w : 18 + 12 * w]


def index_rows(pos_ref, idx_ref):
    idx_ref[...] = jnp.zeros_like(idx_ref)
    for lr in range(12):
        idx_ref[lr : lr + 1, 0:WIN] = pos_ref[lr * 12 : lr * 12 + 1, :]
        idx_ref[16 + lr : 17 + lr, 0:WIN] = pos_ref[lr * 12 + 11 : lr * 12 + 12, :]
    idx_ref[16:32, :] = pltpu.roll(idx_ref[16:32, :], 1, 1)


def disassemble(win_ref, slab_ref, ext_ref):
    for level in range(4):
        for r in range(6):
            k = r % 2
            for w in range(4):
                start = ((level // 2) * 4 + w) * WIN + ((level % 2) * 6 + r) * 12
                slab_ref[k, 6 + 12 * w : 18 + 12 * w, :] = win_ref[start : start + 12, :]
            ext_ref[(level + 1) % 4, r, :, :] = slab_ref[k].astype(BF16)


def attention_window(wi, s):
    rows = pl.ds(pl.multiple_of(wi * WIN, WIN), WIN)
    z = wi // 4
    x = s.x[rows, :]
    normed1, inv1 = norm_stats(x)
    hid = (normed1 * s.n1[...]).astype(BF16)
    s.normed1[rows, :] = normed1
    s.inv1[rows, :] = inv1
    s.hid[rows, :] = hid
    q = (nn(hid, s.wq[0]) * (SCALE * LOG2E)).astype(BF16)
    k = nn(hid, s.wq[1]).astype(BF16)
    v = nn(hid, s.wq[2]).astype(BF16)
    s.k[rows, :] = k
    s.v[rows, :] = v
    qm = spread_heads(q)
    s.q[rows, :] = q
    scores = nt(qm, k)
    b0 = s.bias[0, pl.ds(z * 6, 6)].reshape(864, 128)
    b1 = s.bias[1, pl.ds(z * 6, 6)].reshape(864, 128)
    bias = jnp.concatenate([b0, b1], axis=1)[:, :WIN]
    e = jnp.exp2(scores + bias)
    p = (e * (1.0 / jnp.sum(e, axis=-1, keepdims=True))).astype(BF16)
    s.p[wi] = p
    att = pick_heads(nn(p, v)).astype(BF16)
    s.att[rows, :] = att
    s.blk[rows, :] = x + nn(att, s.wp[...]).astype(BF16).astype(F32)


def mlp_window(wi, s):
    rows = pl.ds(pl.multiple_of(wi * WIN, WIN), WIN)
    mid = s.blk[rows, :]
    normed2, inv2 = norm_stats(mid)
    hid2 = (normed2 * s.n2[...]).astype(BF16)
    s.hid2[rows, :] = hid2
    pre = nn(hid2, s.w1[...])
    u = pre * pre
    t = jnp.tanh(pre * (GELU_K + (GELU_K * GELU_C) * u))
    half = 0.5 + 0.5 * t
    act = pre * half
    slope = half + act * (1.0 - half) * (2.0 * GELU_K + (6.0 * GELU_K * GELU_C) * u)
    act = act.astype(BF16)
    s.act[rows, :] = act
    s.blk[rows, :] = mid + nt(act, s.w2[...])
    cot = s.cot[rows, :]
    d_act = nn(cot.astype(BF16), s.w2[...])
    d_pre = (d_act * slope).astype(BF16)
    s.d_pre[rows, :] = d_pre
    d_hid2 = nt(d_pre, s.w1[...])
    s.gn[1:2, :] += jnp.sum(d_hid2 * normed2, axis=0, keepdims=True)
    s.d_mid[rows, :] = cot + norm_back(d_hid2 * s.n2[...], normed2, inv2)


def backward_window(wi, s):
    rows = pl.ds(pl.multiple_of(wi * WIN, WIN), WIN)
    z = wi // 4
    d_mid = s.d_mid[rows, :]
    d_att = nt(d_mid.astype(BF16), s.wp[...]).astype(BF16)
    dom = spread_heads(d_att)
    v = s.v[rows, :]
    p = s.p[wi]
    d_p = nt(dom, v)
    d_v = tn(p, dom).astype(BF16)
    pf = p.astype(F32)
    pd = pf * d_p
    d_s = pd - pf * jnp.sum(pd, axis=-1, keepdims=True)
    s.d_bias[0, pl.ds(z * 6, 6)] += d_s[:, :128].reshape(6, WIN, 128)
    s.d_bias[1, pl.ds(z * 6, 6), :, 0:16] += d_s[:, 128:].reshape(6, WIN, 16)
    d_low = d_s.astype(BF16)
    d_k = (tn(d_low, spread_heads(s.q[rows, :])) * LN2).astype(BF16)
    d_q = (pick_heads(nn(d_low, s.k[rows, :])) * SCALE).astype(BF16)
    s.dq[rows, :] = d_q
    s.dk[rows, :] = d_k
    s.dv[rows, :] = d_v
    d_win = nt(d_q, s.wq[0]) + nt(d_k, s.wq[1]) + nt(d_v, s.wq[2])
    d_hid = d_win.astype(BF16).astype(F32)
    normed1 = s.normed1[rows, :]
    s.gn[0:1, :] += jnp.sum(d_hid * normed1, axis=0, keepdims=True)
    s.x[rows, :] = d_mid + norm_back(d_hid * s.n1[...], normed1, s.inv1[rows, :])


def table_fold(d_bias_ref, can_ref, start, stop):
    lane = lax.broadcasted_iota(jnp.int32, (12, 256), 1)
    col = lane - (lane // 12) * 12

    def one(zh, carry):
        up = jnp.zeros((12, 256), F32)
        down = jnp.zeros((12, 256), F32)
        for c in range(12):
            x0 = d_bias_ref[0, zh, pl.ds(c, 12, stride=12), :]
            x1 = d_bias_ref[1, zh, pl.ds(c, 12, stride=12), :]
            x = jnp.concatenate([x0, x1], axis=1)
            over = jnp.where(col >= c, x, 0.0)
            up = up + (pltpu.roll(over, 256 - c, 1) if c else over)
            if c:
                down = down + pltpu.roll(x - over, 12 - c, 1)
        can_ref[zh, 0:12, :] = up
        can_ref[zh, 12:24, :] = down
        return carry

    lax.fori_loop(start, stop, one, 0)


def table_entries(idx_ref, sums, can_ref, lhs_ref, tab_ref, out_ref):
    can_ref[0:72, 0:128] = sums[0:72]
    for i in range(8):
        can_ref[9 * i : 9 * i + 9, 128:WIN] = sums[72:81, 16 * i : 16 * i + 16]
    entry = lax.broadcasted_iota(jnp.int32, (128, 256), 0)
    lane = lax.broadcasted_iota(jnp.int32, (1, 256), 1)
    spot = lane - (lane // 12) * 12
    acc = jnp.zeros((26 * 8, 128), F32)
    for part in range(2):
        for lr in range(12):
            idx = idx_ref[part * 16 + lr : part * 16 + lr + 1, :]
            ok = lane < WIN
            if part == 1:
                ok = ok & (spot > 0)
            hi = jnp.where(ok, idx >> 7, 99)
            here = jnp.where(entry == (idx & 127), 1.0, 0.0).astype(BF16)
            at = part * 12 + lr
            d = jnp.concatenate([can_ref[24 * k + at : 24 * k + at + 1, :] for k in range(3)] + [jnp.zeros((5, 256), F32)], axis=0)
            for a in range(26):
                lhs_ref[a * 8 : (a + 1) * 8, :] = jnp.where(hi == a, d, 0.0)
            acc = acc + nt(lhs_ref[...].astype(BF16), here)
    for a in range(26):
        tab_ref[3 * a : 3 * a + 3, :] = acc[8 * a : 8 * a + 3]
    out_ref[...] = tab_ref[0:80, :]


class Refs:
    pass


NAMES = [
    ("wq", (3, C, C), BF16),
    ("bias", (2, 12, WIN, 128), F32),
    ("d_bias", (2, 12, WIN, 128), F32),
    ("x", (TOK, C), F32),
    ("cot", (TOK, C), F32),
    ("blk", (TOK, C), F32),
    ("d_mid", (TOK, C), F32),
    ("normed1", (TOK, C), F32),
    ("inv1", (TOK, 1), F32),
    ("hid", (TOK, C), BF16),
    ("q", (TOK, C), BF16),
    ("k", (TOK, C), BF16),
    ("v", (TOK, C), BF16),
    ("p", (NWIN, 864, WIN), BF16),
    ("att", (TOK, C), BF16),
    ("hid2", (TOK, C), BF16),
    ("act", (TOK, FFN), BF16),
    ("d_pre", (TOK, FFN), BF16),
    ("dq", (TOK, C), BF16),
    ("dk", (TOK, C), BF16),
    ("dv", (TOK, C), BF16),
    ("gn", (8, C), F32),
    ("gall", (C, FFN), F32),
    ("can", (12, 24, 256), F32),
    ("pack", (96, 128), F32),
    ("rest", (72, 16), F32),
    ("idx", (32, 256), jnp.int32),
    ("own_can", (72, 256), F32),
    ("lhs", (26 * 8, 256), F32),
    ("tab", (80, 128), F32),
    ("slab", (2, 64, C), F32),
    ("ext_tok", (4, 6, 64, C), BF16),
    ("ext_cot", (4, 6, 64, C), BF16),
    ("e_blk", (4, 6, 64, C), BF16),
    ("e_tok", (4, 6, 64, C), BF16),
    ("f_own", (2 * C, FFN), BF16),
    ("f_sib", (2 * C, 384), BF16),
    ("f_core", (2 * C, 384), BF16),
    ("f_lon", (8, 48, 384), BF16),
    ("f_lat", (8, 48, 384), BF16),
    ("f_all", (8, 48, 384), BF16),
    ("t_own", (2, 8, 96, 128), BF16),
    ("t_sib", (8, 96, 128), BF16),
    ("t_core", (8, 96, 128), BF16),
    ("t_lon", (8, 96, 128), BF16),
    ("t_lat", (8, 96, 128), BF16),
    ("t_all", (8, 96, 128), BF16),
    ("zone_own", (8, 128), F32),
    ("zone_in", (8, 128), F32),
    ("table_in", (6, 1, POS), F32),
]


def pack_table(s):
    for p in range(12, 16):
        for k in range(3):
            zh = (p - 12) * 3 + k
            s.pack[24 * k : 24 * k + 24, :] = s.can[zh, :, 0:128]
            s.rest[24 * k : 24 * k + 24, :] = s.can[zh, :, 128:WIN]
        for i in range(8):
            s.pack[72:81, 16 * i : 16 * i + 16] = s.rest[9 * i : 9 * i + 9, :]
        s.t_own[p % 2, p // 2, 0:80, :] = s.pack[0:80, :].astype(BF16)
        if p == 12:
            for i in range(2):
                s.pack[88 + 2 * i : 89 + 2 * i, :] = s.gn[i : i + 1, 0:128]
                s.pack[89 + 2 * i : 90 + 2 * i, 0:64] = s.gn[i : i + 1, 128:C]
        else:
            s.pack[88:92, :] = jnp.zeros((4, 128), F32)
        s.t_own[p % 2, p // 2, 80:96, :] = s.pack[80:96, :].astype(BF16)


SEMS = [
    ("local", 16),
    ("in_send", 20),
    ("in_recv", 20),
    ("out_send", 18),
    ("out_recv", 18),
    ("core_send", 5),
    ("core_recv", 5),
] + [(name, 8) for name in ("fa_send", "fa_recv", "fb_send", "fb_recv", "fc_send", "fc_recv",
                            "ta_send", "ta_recv", "tb_send", "tb_recv", "tc_send", "tc_recv")]


def remote(src, dst, send, recv, where):
    return pltpu.make_async_remote_copy(
        src_ref=src, dst_ref=dst, send_sem=send, recv_sem=recv, device_id=where, device_id_type=pl.DeviceIdType.MESH
    )


def each_peer(count, me, start, stop, body):
    def one(p, carry):
        @pl.when(p != me)
        def _():
            body(p)

        return carry

    lax.fori_loop(start, stop, one, 0)


def main_kernel(
    tok, cot, n1, wqkv, wp, table, pos, mask, n2, w1, w2,
    blk_main, blk_cols, gtok_main, gtok_cols, f_res, t_res, *scratch
):
    s = Refs()
    for (name, _, _), ref in zip(NAMES, scratch):
        setattr(s, name, ref)
    for (name, _), ref in zip(SEMS, scratch[len(NAMES) :]):
        setattr(s, name, ref)
    s.n1, s.n2, s.wp, s.w1, s.w2 = n1, n2, wp, w1, w2
    lon = lax.axis_index("lon")
    lat = lax.axis_index("lat")
    lon_up, lon_down = lax.rem(lon + 1, 16), lax.rem(lon + 15, 16)
    lat_up, lat_down = lax.rem(lat + 1, 8), lax.rem(lat + 7, 8)
    chip = lon // 2
    core = lon - 2 * chip
    sibling = {"lon": lon + 1 - 2 * core, "lat": lat}
    barrier = pltpu.get_barrier_semaphore()

    def greet(a, b):
        pl.semaphore_signal(
            barrier, inc=1, device_id={"lon": a, "lat": b}, device_id_type=pl.DeviceIdType.MESH
        )

    for a in (lon_up, lon_down):
        for b in (lat_down, lat, lat_up):
            greet(a, b)
    each_peer(8, lat, 0, 8, lambda p: greet(lon, p))
    each_peer(8, chip, 0, 8, lambda p: greet(2 * p + core, lat))

    spans = ((1, 3), (3, 4), (0, 1))
    locals_in = []
    halo_in = [[], [], [], []]
    for i, (src, dst) in enumerate(((tok, s.ext_tok), (cot, s.ext_cot))):
        for n, (start, stop) in enumerate(spans):
            kept, gone, far = (slice(3, 6), slice(0, 3), lat_down) if n == 0 else (slice(0, 3), slice(3, 6), lat_up)
            a, b = src.at[start:stop], dst.at[start:stop]
            locals_in.append(pltpu.make_async_copy(a.at[:, kept], b.at[:, gone, 0:48], s.local.at[3 * i + n]))
            moves = (
                (a.at[:, gone], b.at[:, kept, 0:48], {"lon": lon, "lat": far}),
                (a.at[:, kept, 0:16], b.at[:, gone, 48:64], {"lon": lon_down, "lat": lat}),
                (a.at[:, gone, 0:16], b.at[:, kept, 48:64], {"lon": lon_down, "lat": far}),
            )
            for k, (a, b, where) in enumerate(moves):
                at = 9 * i + 3 * n + k
                copy = remote(a, b, s.in_send.at[at], s.in_recv.at[at], where)
                halo_in[2 * i + min(n, 1)].append(copy)
    for copy in locals_in:
        copy.start()
    zone_row(mask, s.zone_own)
    up = {"lon": lon, "lat": lat_up}
    table_copy = remote(table.at[6:12], s.table_in, s.in_send.at[18], s.in_recv.at[18], up)
    zone_copy = remote(s.zone_own, s.zone_in, s.in_send.at[19], s.in_recv.at[19], up)
    pl.semaphore_wait(barrier, 20)
    for copy in halo_in[0] + [zone_copy, table_copy] + halo_in[1]:
        copy.start()

    for i in range(3):
        s.wq[i] = wqkv[:, i * C : (i + 1) * C]
    for ref in (s.d_bias, s.gn, s.slab, s.pack, s.own_can, s.tab):
        ref[...] = jnp.zeros_like(ref)
    index_rows(pos, s.idx)
    prep_bias(0, table, s.idx, s.zone_own, s.bias)

    def arrived(group):
        for copy in halo_in[group]:
            copy.wait_recv()

    def window_loop(body, start, stop):
        lax.fori_loop(start, stop, lambda i, c: (body(i, s), c)[1], 0)

    def send_out(i, e, main, cols):
        copies = []
        for n, (start, stop) in enumerate(spans):
            kept, gone, far = (slice(3, 6), slice(0, 3), lat_up) if n == 0 else (slice(0, 3), slice(3, 6), lat_down)
            a, b, c = e.at[start:stop], main.at[start:stop], cols.at[start:stop]
            copy = pltpu.make_async_copy(a.at[:, gone, 0:48], b.at[:, kept], s.local.at[6 + 3 * i + n])
            copy.start()
            waits = [copy.wait]
            moves = (
                (a.at[:, kept, 0:48], b.at[:, gone], {"lon": lon, "lat": far}),
                (a.at[:, gone, 48:64], c.at[:, kept], {"lon": lon_up, "lat": lat}),
                (a.at[:, kept, 48:64], c.at[:, gone], {"lon": lon_up, "lat": far}),
            )
            for k, (a, b, where) in enumerate(moves):
                at = 9 * i + 3 * n + k
                copy = remote(a, b, s.out_send.at[at], s.out_recv.at[at], where)
                copy.start()
                waits += [copy.wait_send, copy.wait_recv]
            copies += waits
        return copies

    def chips_send(src_of, slots, send, recv, start, stop):
        def go(p):
            where = {"lon": 2 * p + core, "lat": lat}
            remote(src_of(p), slots.at[chip], send.at[p], recv.at[chip], where).start()

        each_peer(8, chip, start, stop, go)

    def chips_wait(src_of, slots, send, recv):
        def done(p):
            where = {"lon": 2 * p + core, "lat": lat}
            copy = remote(src_of(p), slots.at[p], send.at[p], recv.at[p], where)
            copy.wait_send()
            copy.wait_recv()

        each_peer(8, chip, 0, 8, done)

    def lat_send(slots, send, recv):
        def go(p):
            remote(slots.at[lat], slots.at[lat], send.at[p], recv.at[lat], {"lon": lon, "lat": p}).start()

        each_peer(8, lat, 0, 8, go)

    def lat_wait(slots, send, recv):
        def done(p):
            copy = remote(slots.at[lat], slots.at[p], send.at[p], recv.at[p], {"lon": lon, "lat": p})
            copy.wait_send()
            copy.wait_recv()

        each_peer(8, lat, 0, 8, done)

    def half(k):
        return pl.ds(pl.multiple_of(k * 384, 384), 384)

    def core_copy(i, src, dst):
        return remote(src, dst, s.core_send.at[i], s.core_recv.at[i], sibling)

    def f_piece(p):
        return s.f_core.at[pl.ds(pl.multiple_of(p * 48, 48), 48), :]

    def t_piece(p):
        return s.t_core.at[p]

    def f_done(p):
        return s.f_all.at[chip]

    def t_done(p):
        return s.t_all.at[chip]

    def total(slots, count):
        acc = slots[0].astype(F32)
        for i in range(1, count):
            acc = acc + slots[i].astype(F32)
        return acc

    def both(i, s):
        attention_window(i + 4, s)
        mlp_window(i, s)

    for copy in halo_in[2] + halo_in[3]:
        copy.start()
    locals_in[0].wait()
    arrived(0)
    assemble(s.ext_tok, s.x, 0)
    window_loop(attention_window, 0, 4)
    table_copy.wait()
    zone_copy.wait()
    prep_bias(1, s.table_in, s.idx, s.zone_in, s.bias)
    for copy in locals_in[1:3]:
        copy.wait()
    arrived(1)
    assemble(s.ext_tok, s.x, 1)
    locals_in[3].wait()
    arrived(2)
    assemble(s.ext_cot, s.cot, 0)
    window_loop(both, 0, 4)
    for copy in locals_in[4:6]:
        copy.wait()
    arrived(3)
    assemble(s.ext_cot, s.cot, 1)
    window_loop(mlp_window, 4, 8)
    for group in halo_in:
        for copy in group:
            copy.wait_send()
    s.f_own[0:C, :] = tn(s.hid2[...], s.d_pre[...]).astype(BF16)
    s.f_own[C : 2 * C, :] = tn(s.cot[...].astype(BF16), s.act[...]).astype(BF16)
    f_swap = core_copy(0, s.f_own.at[:, half(1 - core)], s.f_sib)
    f_swap.start()
    disassemble(s.blk, s.slab, s.e_blk)
    out_waits = send_out(0, s.e_blk, blk_main, blk_cols)
    f_swap.wait()
    s.f_core[...] = (s.f_own[:, half(core)].astype(F32) + s.f_sib[...].astype(F32)).astype(BF16)
    chips_send(f_piece, s.f_lon, s.fa_send, s.fa_recv, 0, 8)
    s.f_lon[chip] = f_piece(chip)[...]

    window_loop(backward_window, 0, 4)
    chips_wait(f_piece, s.f_lon, s.fa_send, s.fa_recv)
    s.f_lat[lat] = total(s.f_lon, 8).astype(BF16)
    lat_send(s.f_lat, s.fb_send, s.fb_recv)
    window_loop(backward_window, 4, 7)
    table_fold(s.d_bias, s.can, 0, 6)
    lat_wait(s.f_lat, s.fb_send, s.fb_recv)
    s.f_all[chip] = total(s.f_lat, 8).astype(BF16)
    chips_send(f_done, s.f_all, s.fc_send, s.fc_recv, 0, 8)
    window_loop(backward_window, 7, NWIN)

    hid = s.hid[...]
    s.gall[:, 0:C] = tn(hid, s.dq[...])
    s.gall[:, C : 2 * C] = tn(hid, s.dk[...])
    s.gall[:, 2 * C : 3 * C] = tn(hid, s.dv[...])
    s.gall[:, 3 * C : 4 * C] = tn(s.att[...], s.d_mid[...].astype(BF16))
    for p in range(12):
        for t in range(6):
            part = s.gall[p * 16 : (p + 1) * 16, t * 128 : (t + 1) * 128]
            s.t_own[p % 2, p // 2, t * 16 : (t + 1) * 16, :] = part.astype(BF16)
    t_swap = core_copy(1, s.t_own.at[1 - core, 0:6], s.t_sib.at[0:6])
    t_swap.start()
    table_fold(s.d_bias, s.can, 6, 12)
    pack_table(s)
    table_swap = core_copy(2, s.t_own.at[1 - core, 6:8], s.t_sib.at[6:8])
    table_swap.start()
    t_swap.wait()
    s.t_core[0:6] = (s.t_own[core, 0:6].astype(F32) + s.t_sib[0:6].astype(F32)).astype(BF16)
    chips_send(t_piece, s.t_lon, s.ta_send, s.ta_recv, 0, 6)
    table_swap.wait()
    s.t_core[6:8] = (s.t_own[core, 6:8].astype(F32) + s.t_sib[6:8].astype(F32)).astype(BF16)
    chips_send(t_piece, s.t_lon, s.ta_send, s.ta_recv, 6, 8)
    s.t_lon[chip] = s.t_core[chip]
    disassemble(s.x, s.slab, s.e_tok)
    out_waits += send_out(1, s.e_tok, gtok_main, gtok_cols)
    chips_wait(t_piece, s.t_lon, s.ta_send, s.ta_recv)
    s.t_lat[lat] = total(s.t_lon, 8).astype(BF16)
    lat_send(s.t_lat, s.tb_send, s.tb_recv)
    chips_wait(f_done, s.f_all, s.fc_send, s.fc_recv)
    f_back = core_copy(3, s.f_all, f_res.at[core])
    f_back.start()
    f_here = pltpu.make_async_copy(s.f_all, f_res.at[core], s.local.at[12])
    f_here.start()
    lat_wait(s.t_lat, s.tb_send, s.tb_recv)
    sums = total(s.t_lat, 8)

    @pl.when(chip < 6)
    def _():
        s.t_all[chip] = sums.astype(BF16)

    @pl.when(chip >= 6)
    def _():
        owner = jnp.where(chip == 7, lat_up, lat)
        table_entries(s.idx, s.t_lat[owner].astype(F32), s.own_can, s.lhs, s.tab, s.pack.at[0:80])
        s.t_all[chip, 0:80] = s.pack[0:80, :].astype(BF16)
        s.t_all[chip, 80:96] = sums[80:96].astype(BF16)

    chips_send(t_done, s.t_all, s.tc_send, s.tc_recv, 0, 8)
    f_back.wait()
    f_here.wait()
    for wait in out_waits:
        wait()
    chips_wait(t_done, s.t_all, s.tc_send, s.tc_recv)
    t_back = core_copy(4, s.t_all, t_res.at[core])
    t_back.start()
    t_here = pltpu.make_async_copy(s.t_all, t_res.at[core], s.local.at[13])
    t_here.start()
    t_back.wait()
    t_here.wait()


def finish_kernel(
    *refs
):
    far, outs, near, (w_full, sem) = refs[:6], refs[6:15], refs[15:21], refs[21:]
    block, gtok, gn1, gqkv, gproj, gtable, gn2, gfc1, gfc2 = outs
    blk_main, blk_cols, gtok_main, gtok_cols, f_res, t_res = near
    copies = [pltpu.make_async_copy(a, b, sem.at[i]) for i, (a, b) in enumerate(zip(far, near))]
    for copy in copies:
        copy.start()
    for copy in copies:
        copy.wait()
    col = lax.broadcasted_iota(jnp.int32, (16, C), 0)
    for main, cols, out in ((blk_main, blk_cols, block), (gtok_main, gtok_cols, gtok)):
        for level in range(4):
            for r in range(6):
                edge = jnp.where(col < 6, cols[level, r].astype(F32), main[level, r, 0:16, :].astype(F32))
                out[level, r, 0:16, :] = edge.astype(BF16)
                out[level, r, 16:48, :] = main[level, r, 16:48, :]
    for p in range(16):
        out = gfc1 if p < 8 else gfc2
        g, half = (p // 2) % 4, p % 2
        out[g * 48 : (g + 1) * 48, half * 384 : (half + 1) * 384] = f_res[p % 2, p // 2].astype(F32) * FACTOR
    for p in range(12):
        for t in range(6):
            part = t_res[p % 2, p // 2, t * 16 : (t + 1) * 16, :].astype(F32) * FACTOR
            w_full[p * 16 : (p + 1) * 16, t * 128 : (t + 1) * 128] = part
    gqkv[...] = w_full[:, 0:576]
    gproj[...] = w_full[:, 576:768]
    for p in range(12, 16):
        tab = t_res[p % 2, p // 2, 0:80, :].astype(F32) * FACTOR
        for a in range(26):
            width = min(128, POS - a * 128)
            for k in range(3):
                gtable[(p - 12) * 3 + k, :, a * 128 : a * 128 + width] = tab[a * 3 + k : a * 3 + k + 1, 0:width]
    norms = t_res[0, 6, 80:96, :].astype(F32) * FACTOR
    for i, out in enumerate((gn1, gn2)):
        out[:, 0:128] = norms[8 + 2 * i : 9 + 2 * i, :]
        out[:, 128:C] = norms[9 + 2 * i : 10 + 2 * i, 0:64]


def shards(tokens, norm1_gain, w_qkv, w_proj, bias_table, pos_index, mask_ids, norm2_gain, w_fc1, w_fc2, cotangent):
    vm = pl.BlockSpec(memory_space=pltpu.VMEM)
    anywhere = pl.BlockSpec(memory_space=pl.ANY)
    main = jax.ShapeDtypeStruct((4, 6, 48, C), BF16)
    cols = jax.ShapeDtypeStruct((4, 6, 16, C), BF16)
    outs = pl.pallas_call(
        main_kernel,
        out_shape=[
            main, cols, main, cols,
            jax.ShapeDtypeStruct((2, 8, 48, 384), BF16),
            jax.ShapeDtypeStruct((2, 8, 96, 128), BF16),
        ],
        in_specs=[anywhere] * 2 + [vm] * 5 + [pl.BlockSpec(memory_space=pltpu.SMEM)] + [vm] * 3,
        out_specs=[anywhere] * 6,
        scratch_shapes=[pltpu.VMEM(shape, dtype) for _, shape, dtype in NAMES]
        + [pltpu.SemaphoreType.DMA((n,)) for _, n in SEMS],
        compiler_params=pltpu.CompilerParams(
            vmem_limit_bytes=56 * 1024 * 1024, collective_id=0, has_side_effects=True
        ),
    )(
        tokens, cotangent, norm1_gain.reshape(1, C), w_qkv, w_proj,
        bias_table.transpose(0, 2, 1, 3).reshape(12, 1, POS), pos_index, mask_ids,
        norm2_gain.reshape(1, C), w_fc1, w_fc2.T,
    )
    f32 = lambda *shape: jax.ShapeDtypeStruct(shape, F32)
    block, gtok, gn1, gqkv, gproj, gtable, gn2, gfc1, gfc2 = pl.pallas_call(
        finish_kernel,
        out_shape=[main, main, f32(1, C), f32(C, 576), f32(C, C), f32(12, 1, POS), f32(1, C), f32(C, FFN), f32(C, FFN)],
        in_specs=[anywhere] * 6,
        out_specs=[vm] * 9,
        scratch_shapes=[pltpu.VMEM(out.shape, out.dtype) for out in outs]
        + [pltpu.VMEM((C, FFN), F32), pltpu.SemaphoreType.DMA((6,))],
        compiler_params=pltpu.CompilerParams(vmem_limit_bytes=56 * 1024 * 1024),
    )(*outs)
    gtable = gtable.reshape(2, 6, 1, POS).transpose(0, 2, 1, 3)
    return (block, gtok, gn1.reshape(C), gqkv, gproj, gtable, gn2.reshape(C), gfc1, gfc2.T)


def solution(mesh):
    act = P(None, "lat", "lon", None)
    table = P(None, "lat", None, None)
    return jax.shard_map(
        shards,
        mesh=mesh,
        in_specs=(act, P(), P(), P(), table, P(), P("lat"), P(), P(), P(), act),
        out_specs=(act, act, P(), P(), P(), table, P(), P(), P()),
        check_vma=False,
    )
```

```python
import jax
import jax.numpy as jnp
from jax import lax
from jax.experimental import pallas as pl
from jax.experimental.pallas import tpu as pltpu
from jax.sharding import PartitionSpec as P

F32 = jnp.float32
BF16 = jnp.bfloat16
C = 192
HEADS = 6
FFN = 768
WIN = 144
NWIN = 8
TOK = 1152
POS = 3312
EPS = 1e-05
GELU_K = 0.7978845608
GELU_C = 0.044715
LOG2E = 1.4426950408889634
LN2 = 0.6931471805599453
SCALE = 32 ** -0.5
FACTOR = 147456.0 ** -0.5


def nn(a, b):
    return lax.dot_general(a, b, (((1,), (0,)), ((), ())), preferred_element_type=F32)


def nt(a, b):
    return lax.dot_general(a, b, (((1,), (1,)), ((), ())), preferred_element_type=F32)


def tn(a, b):
    return lax.dot_general(a, b, (((0,), (0,)), ((), ())), preferred_element_type=F32)


def head_mask(h, dtype):
    lane = lax.broadcasted_iota(jnp.int32, (1, C), 1)
    inside = (lane >= h * 32) & (lane < h * 32 + 32)
    return jnp.where(inside, 1.0, 0.0).astype(dtype)


def spread_heads(x):
    return jnp.concatenate([x * head_mask(h, BF16) for h in range(HEADS)], axis=0)


def pick_heads(x):
    total = x[:WIN] * head_mask(0, F32)
    for h in range(1, HEADS):
        total = total + x[h * WIN : (h + 1) * WIN] * head_mask(h, F32)
    return total


def mean_of(x):
    return jnp.sum(x, axis=-1, keepdims=True) * (1.0 / C)


def norm_stats(x):
    center = x - mean_of(x)
    inv = lax.rsqrt(mean_of(center * center) + EPS)
    return center * inv, inv


def norm_back(g, normed, inv):
    return inv * (g - mean_of(g) - normed * mean_of(g * normed))


def zone_row(mask_ref, out_ref):
    lane = lax.broadcasted_iota(jnp.int32, (8, 128), 1)
    ids = jnp.zeros((8, 128), jnp.int32)
    for r in range(6):
        ids = jnp.where(lane == r, 2 * mask_ref[r], ids)
    out_ref[...] = ids.astype(F32)


def prep_bias(z, table_ref, idx_ref, zone_ref, bias_ref):
    sub = lax.broadcasted_iota(jnp.int32, (16, 256), 0)
    lane = lax.broadcasted_iota(jnp.int32, (16, 256), 1)
    lane_row = lane // 12
    col = lane - lane_row * 12
    top_i = jnp.where(sub >= 6, 1, 0)
    top_j = jnp.where(lane_row >= 6, 1, 0)
    row_i = sub - 6 * top_i
    row_j = lane_row - 6 * top_j
    zone_i = top_i.astype(F32) if z == 1 else jnp.zeros((16, 256), F32)
    zone_j = top_j.astype(F32) if z == 1 else jnp.zeros((16, 256), F32)
    for r in range(6):
        here = jnp.broadcast_to(zone_ref[0:1, r : r + 1], (16, 256))
        zone_i = zone_i + jnp.where(row_i == r, here, 0.0)
        zone_j = zone_j + jnp.where(row_j == r, here, 0.0)
    mask = jnp.where(zone_i == zone_j, 0.0, -1e30)
    idx = idx_ref[...]
    hi = idx >> 7
    lo = idx & 127

    def one(h, carry):
        row = table_ref[h] * LOG2E
        tiles = []
        for t in range(2):
            lo_t = lo[:, t * 128 : (t + 1) * 128]
            hi_t = hi[:, t * 128 : (t + 1) * 128]
            acc = jnp.zeros((32, 128), F32)
            for a in range(26):
                part = row[:, a * 128 : min(POS, (a + 1) * 128)]
                if a == 25:
                    part = jnp.concatenate([part, jnp.zeros((1, 16), F32)], axis=1)
                got = jnp.take_along_axis(jnp.broadcast_to(part, (32, 128)), lo_t, axis=1)
                acc = jnp.where(hi_t == a, got, acc)
            tiles.append(acc)
        both = jnp.concatenate(tiles, axis=1)
        upper, lower = both[:16], both[16:]
        for c in range(12):
            ahead = pltpu.roll(upper, c, 1) if c else upper
            val = jnp.where(col >= c, ahead, pltpu.roll(lower, 256 - 12 + c, 1)) + mask
            bias_ref[0, 6 * z + h, pl.ds(c, 12, stride=12), :] = val[:12, :128]
            bias_ref[1, 6 * z + h, pl.ds(c, 12, stride=12), :] = val[:12, 128:]
        return carry

    lax.fori_loop(0, 6, one, 0)


def assemble(ext_ref, win_ref, z):
    for level in (2 * z, 2 * z + 1):
        for r in range(6):
            slab = ext_ref[(level + 1) % 4, r, :, :].astype(F32)
            for w in range(4):
                start = (z * 4 + w) * WIN + ((level % 2) * 6 + r) * 12
                win_ref[start : start + 12, :] = slab[6 + 12 * w : 18 + 12 * w]


def index_rows(pos_ref, idx_ref):
    idx_ref[...] = jnp.zeros_like(idx_ref)
    for lr in range(12):
        idx_ref[lr : lr + 1, 0:WIN] = pos_ref[lr * 12 : lr * 12 + 1, :]
        idx_ref[16 + lr : 17 + lr, 0:WIN] = pos_ref[lr * 12 + 11 : lr * 12 + 12, :]
    idx_ref[16:32, :] = pltpu.roll(idx_ref[16:32, :], 1, 1)


def disassemble(win_ref, slab_ref, ext_ref):
    for level in range(4):
        for r in range(6):
            k = r % 2
            for w in range(4):
                start = ((level // 2) * 4 + w) * WIN + ((level % 2) * 6 + r) * 12
                slab_ref[k, 6 + 12 * w : 18 + 12 * w, :] = win_ref[start : start + 12, :]
            ext_ref[(level + 1) % 4, r, :, :] = slab_ref[k].astype(BF16)


def attention_window(wi, s):
    rows = slice(wi * WIN, (wi + 1) * WIN)
    z = wi // 4
    x = s.x[rows, :]
    normed1, inv1 = norm_stats(x)
    hid = (normed1 * s.n1[...]).astype(BF16)
    s.normed1[rows, :] = normed1
    s.inv1[rows, :] = inv1
    s.hid[rows, :] = hid
    q = (nn(hid, s.wq[0]) * (SCALE * LOG2E)).astype(BF16)
    k = nn(hid, s.wq[1]).astype(BF16)
    v = nn(hid, s.wq[2]).astype(BF16)
    s.k[rows, :] = k
    s.v[rows, :] = v
    qm = spread_heads(q)
    s.q[rows, :] = q
    scores = nt(qm, k)
    b0 = s.bias[0, 6 * z : 6 * z + 6].reshape(864, 128)
    b1 = s.bias[1, 6 * z : 6 * z + 6].reshape(864, 128)
    bias = jnp.concatenate([b0, b1], axis=1)[:, :WIN]
    e = jnp.exp2(scores + bias)
    p = (e * (1.0 / jnp.sum(e, axis=-1, keepdims=True))).astype(BF16)
    s.p[wi] = p
    att = pick_heads(nn(p, v)).astype(BF16)
    s.att[rows, :] = att
    s.blk[rows, :] = x + nn(att, s.wp[...]).astype(BF16).astype(F32)


def mlp_window(wi, s):
    rows = slice(wi * WIN, (wi + 1) * WIN)
    mid = s.blk[rows, :]
    normed2, inv2 = norm_stats(mid)
    hid2 = (normed2 * s.n2[...]).astype(BF16)
    s.hid2[rows, :] = hid2
    pre = nn(hid2, s.w1[...])
    u = pre * pre
    t = jnp.tanh(pre * (GELU_K + (GELU_K * GELU_C) * u))
    half = 0.5 + 0.5 * t
    act = pre * half
    slope = half + act * (1.0 - half) * (2.0 * GELU_K + (6.0 * GELU_K * GELU_C) * u)
    act = act.astype(BF16)
    s.act[rows, :] = act
    s.blk[rows, :] = mid + nt(act, s.w2[...])
    cot = s.cot[rows, :]
    d_act = nn(cot.astype(BF16), s.w2[...])
    d_pre = (d_act * slope).astype(BF16)
    s.d_pre[rows, :] = d_pre
    d_hid2 = nt(d_pre, s.w1[...])
    s.gn[1:2, :] += jnp.sum(d_hid2 * normed2, axis=0, keepdims=True)
    s.d_mid[rows, :] = cot + norm_back(d_hid2 * s.n2[...], normed2, inv2)


def backward_window(wi, s):
    rows = slice(wi * WIN, (wi + 1) * WIN)
    z = wi // 4
    d_mid = s.d_mid[rows, :]
    d_att = nt(d_mid.astype(BF16), s.wp[...]).astype(BF16)
    dom = spread_heads(d_att)
    v = s.v[rows, :]
    p = s.p[wi]
    d_p = nt(dom, v)
    d_v = tn(p, dom).astype(BF16)
    pf = p.astype(F32)
    pd = pf * d_p
    d_s = pd - pf * jnp.sum(pd, axis=-1, keepdims=True)
    d_s0, d_s1 = d_s[:, :128].reshape(6, WIN, 128), d_s[:, 128:].reshape(6, WIN, 16)
    if wi % 4:
        d_s0 = d_s0 + s.d_bias[0, 6 * z : 6 * z + 6]
        d_s1 = d_s1 + s.d_bias[1, 6 * z : 6 * z + 6, :, 0:16]
    s.d_bias[0, 6 * z : 6 * z + 6] = d_s0
    s.d_bias[1, 6 * z : 6 * z + 6, :, 0:16] = d_s1
    d_low = d_s.astype(BF16)
    d_k = (tn(d_low, spread_heads(s.q[rows, :])) * LN2).astype(BF16)
    d_q = (pick_heads(nn(d_low, s.k[rows, :])) * SCALE).astype(BF16)
    s.dq[rows, :] = d_q
    s.dk[rows, :] = d_k
    s.dv[rows, :] = d_v
    d_win = nt(d_q, s.wq[0]) + nt(d_k, s.wq[1]) + nt(d_v, s.wq[2])
    d_hid = d_win.astype(BF16).astype(F32)
    normed1 = s.normed1[rows, :]
    s.gn[0:1, :] += jnp.sum(d_hid * normed1, axis=0, keepdims=True)
    s.x[rows, :] = d_mid + norm_back(d_hid * s.n1[...], normed1, s.inv1[rows, :])


def table_fold(d_bias_ref, can_ref, start, stop):
    lane = lax.broadcasted_iota(jnp.int32, (12, 256), 1)
    col = lane - (lane // 12) * 12

    def one(zh, carry):
        up = jnp.zeros((12, 256), F32)
        down = jnp.zeros((12, 256), F32)
        for c in range(12):
            x0 = d_bias_ref[0, zh, pl.ds(c, 12, stride=12), :]
            x1 = d_bias_ref[1, zh, pl.ds(c, 12, stride=12), :]
            x = jnp.where(lane < WIN, jnp.concatenate([x0, x1], axis=1), 0.0)
            over = jnp.where(col >= c, x, 0.0)
            up = up + (pltpu.roll(over, 256 - c, 1) if c else over)
            if c:
                down = down + pltpu.roll(x - over, 12 - c, 1)
        can_ref[zh, 0:12, :] = up
        can_ref[zh, 12:24, :] = down
        return carry

    lax.fori_loop(start, stop, one, 0)


def table_entries(idx_ref, sums, can_ref, lhs_ref, tab_ref, out_ref):
    can_ref[0:72, 0:128] = sums[0:72]
    for i in range(8):
        can_ref[9 * i : 9 * i + 9, 128:WIN] = sums[72:81, 16 * i : 16 * i + 16]
    entry = lax.broadcasted_iota(jnp.int32, (128, 256), 0)
    lane = lax.broadcasted_iota(jnp.int32, (1, 256), 1)
    spot = lane - (lane // 12) * 12
    acc = jnp.zeros((26 * 8, 128), F32)
    for part in range(2):
        for lr in range(12):
            idx = idx_ref[part * 16 + lr : part * 16 + lr + 1, :]
            ok = lane < WIN
            if part == 1:
                ok = ok & (spot > 0)
            hi = jnp.where(ok, idx >> 7, 99)
            here = jnp.where(entry == (idx & 127), 1.0, 0.0).astype(BF16)
            at = part * 12 + lr
            d = jnp.concatenate([can_ref[24 * k + at : 24 * k + at + 1, :] for k in range(3)] + [jnp.zeros((5, 256), F32)], axis=0)
            for a in range(26):
                lhs_ref[a * 8 : (a + 1) * 8, :] = jnp.where(hi == a, d, 0.0)
            acc = acc + nt(lhs_ref[...].astype(BF16), here)
    for a in range(26):
        tab_ref[3 * a : 3 * a + 3, :] = acc[8 * a : 8 * a + 3]
    out_ref[...] = tab_ref[0:80, :]


class Refs:
    pass


NAMES = [
    ("wq", (3, C, C), BF16),
    ("n1", (1, C), F32),
    ("wqkv", (C, 576), BF16),
    ("wp", (C, C), BF16),
    ("table", (12, 1, POS), F32),
    ("pos", (WIN, WIN), jnp.int32),
    ("n2", (1, C), F32),
    ("w1", (C, FFN), BF16),
    ("w2", (C, FFN), BF16),
    ("bias", (2, 12, WIN, 128), F32),
    ("d_bias", (2, 12, WIN, 128), F32),
    ("x", (TOK, C), F32),
    ("cot", (TOK, C), F32),
    ("blk", (TOK, C), F32),
    ("d_mid", (TOK, C), F32),
    ("normed1", (TOK, C), F32),
    ("inv1", (TOK, 1), F32),
    ("hid", (TOK, C), BF16),
    ("q", (TOK, C), BF16),
    ("k", (TOK, C), BF16),
    ("v", (TOK, C), BF16),
    ("p", (NWIN, 864, WIN), BF16),
    ("att", (TOK, C), BF16),
    ("hid2", (TOK, C), BF16),
    ("act", (TOK, FFN), BF16),
    ("d_pre", (TOK, FFN), BF16),
    ("dq", (TOK, C), BF16),
    ("dk", (TOK, C), BF16),
    ("dv", (TOK, C), BF16),
    ("gn", (8, C), F32),
    ("gall", (C, FFN), F32),
    ("can", (12, 24, 256), F32),
    ("pack", (96, 128), F32),
    ("rest", (72, 16), F32),
    ("idx", (32, 256), jnp.int32),
    ("own_can", (72, 256), F32),
    ("lhs", (26 * 8, 256), F32),
    ("tab", (80, 128), F32),
    ("slab", (2, 64, C), F32),
    ("ext_tok", (4, 6, 64, C), BF16),
    ("ext_cot", (4, 6, 64, C), BF16),
    ("e_blk", (4, 6, 64, C), BF16),
    ("e_tok", (4, 6, 64, C), BF16),
    ("f_own", (2 * C, FFN), BF16),
    ("f_sib", (2 * C, 384), BF16),
    ("f_core", (2 * C, 384), BF16),
    ("f_lat", (8, 48, 384), BF16),
    ("f_lon", (8, 48, 384), BF16),
    ("f_all", (8, 48, 384), BF16),
    ("t_own", (2, 8, 96, 128), BF16),
    ("t_sib", (8, 96, 128), BF16),
    ("t_core", (8, 96, 128), BF16),
    ("t_lon", (8, 96, 128), BF16),
    ("t_lat", (8, 96, 128), BF16),
    ("t_all", (8, 96, 128), BF16),
    ("zone_own", (8, 128), F32),
    ("zone_in", (8, 128), F32),
    ("table_in", (6, 1, POS), F32),
]


def pack_table(s):
    for p in range(12, 16):
        for k in range(3):
            zh = (p - 12) * 3 + k
            s.pack[24 * k : 24 * k + 24, :] = s.can[zh, :, 0:128]
            s.rest[24 * k : 24 * k + 24, :] = s.can[zh, :, 128:WIN]
        for i in range(8):
            s.pack[72:81, 16 * i : 16 * i + 16] = s.rest[9 * i : 9 * i + 9, :]
        s.t_own[p % 2, p // 2, 0:80, :] = s.pack[0:80, :].astype(BF16)
        if p == 12:
            for i in range(2):
                s.pack[88 + 2 * i : 89 + 2 * i, :] = s.gn[i : i + 1, 0:128]
                s.pack[89 + 2 * i : 90 + 2 * i, 0:64] = s.gn[i : i + 1, 128:C]
        else:
            s.pack[88:92, :] = jnp.zeros((4, 128), F32)
        s.t_own[p % 2, p // 2, 80:96, :] = s.pack[80:96, :].astype(BF16)


SEMS = [
    ("local", 24),
    ("in_send", 20),
    ("in_recv", 20),
    ("out_send", 18),
    ("out_recv", 18),
    ("core_send", 5),
    ("core_recv", 5),
] + [(name, 8) for name in ("fa_send", "fa_recv", "fb_send", "fb_recv", "fc_send", "fc_recv",
                            "ta_send", "ta_recv", "tb_send", "tb_recv", "tc_send", "tc_recv")]


def remote(src, dst, send, recv, where):
    return pltpu.make_async_remote_copy(
        src_ref=src, dst_ref=dst, send_sem=send, recv_sem=recv, device_id=where, device_id_type=pl.DeviceIdType.MESH
    )


def each_peer(count, me, start, stop, body):
    def one(p, carry):
        @pl.when(p != me)
        def _():
            body(p)

        return carry

    lax.fori_loop(start, stop, one, 0)


def main_kernel(
    tok, cot, n1, wqkv, wp, table, pos, mask, n2, w1, w2,
    blk_main, blk_cols, gtok_main, gtok_cols, f_res, t_res, *scratch
):
    s = Refs()
    for (name, _, _), ref in zip(NAMES, scratch):
        setattr(s, name, ref)
    for (name, _), ref in zip(SEMS, scratch[len(NAMES) :]):
        setattr(s, name, ref)
    fetched = {}
    for i, (name, ref) in enumerate(
        (("pos", pos), ("table", table), ("wqkv", wqkv), ("n1", n1), ("wp", wp), ("n2", n2), ("w1", w1), ("w2", w2))
    ):
        fetched[name] = pltpu.make_async_copy(ref, getattr(s, name), s.local.at[14 + i])
    lon = lax.axis_index("lon")
    lat = lax.axis_index("lat")
    lon_up, lon_down = lax.rem(lon + 1, 16), lax.rem(lon + 15, 16)
    lat_up, lat_down = lax.rem(lat + 1, 8), lax.rem(lat + 7, 8)
    chip = lon // 2
    core = lon - 2 * chip
    sibling = {"lon": lon + 1 - 2 * core, "lat": lat}
    barrier = pltpu.get_barrier_semaphore()
    for name in ("pos", "table", "wqkv"):
        fetched[name].start()

    def greet(a, b):
        pl.semaphore_signal(
            barrier, inc=1, device_id={"lon": a, "lat": b}, device_id_type=pl.DeviceIdType.MESH
        )

    for a in (lon_up, lon_down):
        for b in (lat_down, lat, lat_up):
            greet(a, b)
    each_peer(8, lat, 0, 8, lambda p: greet(lon, p))
    each_peer(8, chip, 0, 8, lambda p: greet(2 * p + core, lat))

    spans = ((1, 3), (3, 4), (0, 1))
    locals_in = []
    halo_in = [[], [], [], []]
    for i, (src, dst) in enumerate(((tok, s.ext_tok), (cot, s.ext_cot))):
        for n, (start, stop) in enumerate(spans):
            kept, gone, far = (slice(3, 6), slice(0, 3), lat_down) if n == 0 else (slice(0, 3), slice(3, 6), lat_up)
            a, b = src.at[start:stop], dst.at[start:stop]
            locals_in.append(pltpu.make_async_copy(a.at[:, kept], b.at[:, gone, 0:48], s.local.at[3 * i + n]))
            moves = (
                (a.at[:, gone], b.at[:, kept, 0:48], {"lon": lon, "lat": far}),
                (a.at[:, kept, 0:16], b.at[:, gone, 48:64], {"lon": lon_down, "lat": lat}),
                (a.at[:, gone, 0:16], b.at[:, kept, 48:64], {"lon": lon_down, "lat": far}),
            )
            for k, (a, b, where) in enumerate(moves):
                at = 9 * i + 3 * n + k
                copy = remote(a, b, s.in_send.at[at], s.in_recv.at[at], where)
                halo_in[2 * i + min(n, 1)].append(copy)
    for copy in locals_in:
        copy.start()
    zone_row(mask, s.zone_own)
    up = {"lon": lon, "lat": lat_up}
    table_copy = remote(table.at[6:12], s.table_in, s.in_send.at[18], s.in_recv.at[18], up)
    zone_copy = remote(s.zone_own, s.zone_in, s.in_send.at[19], s.in_recv.at[19], up)
    pl.semaphore_wait(barrier, 20)
    for copy in halo_in[0] + [zone_copy, table_copy] + halo_in[1]:
        copy.start()

    for name in ("n1", "wp", "n2", "w1", "w2"):
        fetched[name].start()
    fetched["wqkv"].wait()
    for i in range(3):
        s.wq[i] = s.wqkv[:, i * C : (i + 1) * C]
    for ref in (s.gn, s.slab, s.pack, s.own_can, s.tab):
        ref[...] = jnp.zeros_like(ref)
    fetched["pos"].wait()
    index_rows(s.pos, s.idx)
    fetched["table"].wait()
    for name in ("n1", "wp", "n2", "w1", "w2"):
        fetched[name].wait()
    prep_bias(0, s.table, s.idx, s.zone_own, s.bias)

    def arrived(group):
        for copy in halo_in[group]:
            copy.wait_recv()

    def window_loop(body, start, stop):
        for i in range(start, stop):
            body(i, s)

    def send_out(i, e, main, cols):
        copies = []
        for n, (start, stop) in enumerate(spans):
            kept, gone, far = (slice(3, 6), slice(0, 3), lat_up) if n == 0 else (slice(0, 3), slice(3, 6), lat_down)
            a, b, c = e.at[start:stop], main.at[start:stop], cols.at[start:stop]
            copy = pltpu.make_async_copy(a.at[:, gone, 0:48], b.at[:, kept], s.local.at[6 + 3 * i + n])
            copy.start()
            waits = [copy.wait]
            moves = (
                (a.at[:, kept, 0:48], b.at[:, gone], {"lon": lon, "lat": far}),
                (a.at[:, gone, 48:64], c.at[:, kept], {"lon": lon_up, "lat": lat}),
                (a.at[:, kept, 48:64], c.at[:, gone], {"lon": lon_up, "lat": far}),
            )
            for k, (a, b, where) in enumerate(moves):
                at = 9 * i + 3 * n + k
                copy = remote(a, b, s.out_send.at[at], s.out_recv.at[at], where)
                copy.start()
                waits += [copy.wait_send, copy.wait_recv]
            copies += waits
        return copies

    def chips_send(src_of, slots, send, recv, start, stop):
        def go(p):
            where = {"lon": 2 * p + core, "lat": lat}
            remote(src_of(p), slots.at[chip], send.at[p], recv.at[chip], where).start()

        each_peer(8, chip, start, stop, go)

    def chips_wait(src_of, slots, send, recv):
        def done(p):
            where = {"lon": 2 * p + core, "lat": lat}
            copy = remote(src_of(p), slots.at[p], send.at[p], recv.at[p], where)
            copy.wait_send()
            copy.wait_recv()

        each_peer(8, chip, 0, 8, done)

    def lat_send(src_of, slots, send, recv):
        def go(p):
            remote(src_of(p), slots.at[lat], send.at[p], recv.at[lat], {"lon": lon, "lat": p}).start()

        each_peer(8, lat, 0, 8, go)

    def lat_wait(src_of, slots, send, recv):
        def done(p):
            copy = remote(src_of(p), slots.at[p], send.at[p], recv.at[p], {"lon": lon, "lat": p})
            copy.wait_send()
            copy.wait_recv()

        each_peer(8, lat, 0, 8, done)

    def half(k):
        return pl.ds(pl.multiple_of(k * 384, 384), 384)

    def core_copy(i, src, dst):
        return remote(src, dst, s.core_send.at[i], s.core_recv.at[i], sibling)

    def f_piece(p):
        return s.f_core.at[pl.ds(pl.multiple_of(p * 48, 48), 48), :]

    def t_piece(p):
        return s.t_core.at[p]

    def f_done(p):
        return s.f_all.at[lat]

    def f_part(p):
        return s.f_lon.at[chip]

    def t_part(p):
        return s.t_lat.at[lat]

    def t_done(p):
        return s.t_all.at[chip]

    def total(slots, count):
        acc = slots[0].astype(F32)
        for i in range(1, count):
            acc = acc + slots[i].astype(F32)
        return acc

    def both(i, s):
        attention_window(i + 4, s)
        mlp_window(i, s)

    for copy in halo_in[2] + halo_in[3]:
        copy.start()
    locals_in[0].wait()
    arrived(0)
    assemble(s.ext_tok, s.x, 0)
    window_loop(attention_window, 0, 4)
    table_copy.wait()
    zone_copy.wait()
    prep_bias(1, s.table_in, s.idx, s.zone_in, s.bias)
    for copy in locals_in[1:3]:
        copy.wait()
    arrived(1)
    assemble(s.ext_tok, s.x, 1)
    locals_in[3].wait()
    arrived(2)
    assemble(s.ext_cot, s.cot, 0)
    window_loop(both, 0, 4)
    for copy in locals_in[4:6]:
        copy.wait()
    arrived(3)
    assemble(s.ext_cot, s.cot, 1)
    window_loop(mlp_window, 4, 8)
    for group in halo_in:
        for copy in group:
            copy.wait_send()
    s.f_own[0:C, :] = tn(s.hid2[...], s.d_pre[...]).astype(BF16)
    s.f_own[C : 2 * C, :] = tn(s.cot[...].astype(BF16), s.act[...]).astype(BF16)
    f_swap = core_copy(0, s.f_own.at[:, half(1 - core)], s.f_sib)
    f_swap.start()
    disassemble(s.blk, s.slab, s.e_blk)
    f_swap.wait()
    s.f_core[...] = (s.f_own[:, half(core)].astype(F32) + s.f_sib[...].astype(F32)).astype(BF16)
    lat_send(f_piece, s.f_lat, s.fa_send, s.fa_recv)
    s.f_lat[lat] = f_piece(lat)[...]

    window_loop(backward_window, 0, 4)
    lat_wait(f_piece, s.f_lat, s.fa_send, s.fa_recv)
    s.f_lon[chip] = total(s.f_lat, 8).astype(BF16)
    chips_send(f_part, s.f_lon, s.fb_send, s.fb_recv, 0, 8)
    out_waits = send_out(0, s.e_blk, blk_main, blk_cols)
    table_fold(s.d_bias, s.can, 0, 6)
    window_loop(backward_window, 4, NWIN)
    chips_wait(f_part, s.f_lon, s.fb_send, s.fb_recv)
    s.f_all[lat] = total(s.f_lon, 8).astype(BF16)
    lat_send(f_done, s.f_all, s.fc_send, s.fc_recv)

    hid = s.hid[...]
    s.gall[:, 0:C] = tn(hid, s.dq[...])
    s.gall[:, C : 2 * C] = tn(hid, s.dk[...])
    s.gall[:, 2 * C : 3 * C] = tn(hid, s.dv[...])
    s.gall[:, 3 * C : 4 * C] = tn(s.att[...], s.d_mid[...].astype(BF16))
    for p in range(12):
        for t in range(6):
            part = s.gall[p * 16 : (p + 1) * 16, t * 128 : (t + 1) * 128]
            s.t_own[p % 2, p // 2, t * 16 : (t + 1) * 16, :] = part.astype(BF16)
    t_swap = core_copy(1, s.t_own.at[1 - core, 0:6], s.t_sib.at[0:6])
    t_swap.start()
    table_fold(s.d_bias, s.can, 6, 12)
    pack_table(s)
    table_swap = core_copy(2, s.t_own.at[1 - core, 6:8], s.t_sib.at[6:8])
    table_swap.start()
    t_swap.wait()
    s.t_core[0:6] = (s.t_own[core, 0:6].astype(F32) + s.t_sib[0:6].astype(F32)).astype(BF16)
    chips_send(t_piece, s.t_lon, s.ta_send, s.ta_recv, 0, 6)
    table_swap.wait()
    s.t_core[6:8] = (s.t_own[core, 6:8].astype(F32) + s.t_sib[6:8].astype(F32)).astype(BF16)
    chips_send(t_piece, s.t_lon, s.ta_send, s.ta_recv, 6, 8)
    s.t_lon[chip] = s.t_core[chip]
    disassemble(s.x, s.slab, s.e_tok)
    out_waits += send_out(1, s.e_tok, gtok_main, gtok_cols)
    chips_wait(t_piece, s.t_lon, s.ta_send, s.ta_recv)
    s.t_lat[lat] = total(s.t_lon, 8).astype(BF16)
    lat_send(t_part, s.t_lat, s.tb_send, s.tb_recv)
    lat_wait(f_done, s.f_all, s.fc_send, s.fc_recv)
    f_back = core_copy(3, s.f_all, f_res.at[core])
    f_back.start()
    f_here = pltpu.make_async_copy(s.f_all, f_res.at[core], s.local.at[12])
    f_here.start()
    lat_wait(t_part, s.t_lat, s.tb_send, s.tb_recv)
    sums = total(s.t_lat, 8)

    @pl.when(chip < 6)
    def _():
        s.t_all[chip] = sums.astype(BF16)

    @pl.when(chip >= 6)
    def _():
        owner = jnp.where(chip == 7, lat_up, lat)
        table_entries(s.idx, s.t_lat[owner].astype(F32), s.own_can, s.lhs, s.tab, s.pack.at[0:80])
        s.t_all[chip, 0:80] = s.pack[0:80, :].astype(BF16)
        s.t_all[chip, 80:96] = sums[80:96].astype(BF16)

    chips_send(t_done, s.t_all, s.tc_send, s.tc_recv, 0, 8)
    f_back.wait()
    f_here.wait()
    for wait in out_waits:
        wait()
    chips_wait(t_done, s.t_all, s.tc_send, s.tc_recv)
    t_back = core_copy(4, s.t_all, t_res.at[core])
    t_back.start()
    t_here = pltpu.make_async_copy(s.t_all, t_res.at[core], s.local.at[13])
    t_here.start()
    t_back.wait()
    t_here.wait()


def finish_kernel(
    *refs
):
    far, outs, near, (w_full, sem) = refs[:6], refs[6:15], refs[15:21], refs[21:]
    block, gtok, gn1, gqkv, gproj, gtable, gn2, gfc1, gfc2 = outs
    blk_main, blk_cols, gtok_main, gtok_cols, f_res, t_res = near
    copies = [pltpu.make_async_copy(a, b, sem.at[i]) for i, (a, b) in enumerate(zip(far, near))]
    for copy in copies:
        copy.start()
    for copy in copies:
        copy.wait()
    col = lax.broadcasted_iota(jnp.int32, (16, C), 0)
    for main, cols, out in ((blk_main, blk_cols, block), (gtok_main, gtok_cols, gtok)):
        for level in range(4):
            for r in range(6):
                edge = jnp.where(col < 6, cols[level, r].astype(F32), main[level, r, 0:16, :].astype(F32))
                out[level, r, 0:16, :] = edge.astype(BF16)
                out[level, r, 16:48, :] = main[level, r, 16:48, :]
    for p in range(16):
        out = gfc1 if p < 8 else gfc2
        g, half = (p // 2) % 4, p % 2
        out[g * 48 : (g + 1) * 48, half * 384 : (half + 1) * 384] = f_res[p % 2, p // 2].astype(F32) * FACTOR
    for p in range(12):
        for t in range(6):
            part = t_res[p % 2, p // 2, t * 16 : (t + 1) * 16, :].astype(F32) * FACTOR
            w_full[p * 16 : (p + 1) * 16, t * 128 : (t + 1) * 128] = part
    gqkv[...] = w_full[:, 0:576]
    gproj[...] = w_full[:, 576:768]
    for p in range(12, 16):
        tab = t_res[p % 2, p // 2, 0:80, :].astype(F32) * FACTOR
        for a in range(26):
            width = min(128, POS - a * 128)
            for k in range(3):
                gtable[(p - 12) * 3 + k, :, a * 128 : a * 128 + width] = tab[a * 3 + k : a * 3 + k + 1, 0:width]
    norms = t_res[0, 6, 80:96, :].astype(F32) * FACTOR
    for i, out in enumerate((gn1, gn2)):
        out[:, 0:128] = norms[8 + 2 * i : 9 + 2 * i, :]
        out[:, 128:C] = norms[9 + 2 * i : 10 + 2 * i, 0:64]


def shards(tokens, norm1_gain, w_qkv, w_proj, bias_table, pos_index, mask_ids, norm2_gain, w_fc1, w_fc2, cotangent):
    vm = pl.BlockSpec(memory_space=pltpu.VMEM)
    anywhere = pl.BlockSpec(memory_space=pl.ANY)
    main = jax.ShapeDtypeStruct((4, 6, 48, C), BF16)
    cols = jax.ShapeDtypeStruct((4, 6, 16, C), BF16)
    outs = pl.pallas_call(
        main_kernel,
        out_shape=[
            main, cols, main, cols,
            jax.ShapeDtypeStruct((2, 8, 48, 384), BF16),
            jax.ShapeDtypeStruct((2, 8, 96, 128), BF16),
        ],
        in_specs=[anywhere] * 7 + [pl.BlockSpec(memory_space=pltpu.SMEM)] + [anywhere] * 3,
        out_specs=[anywhere] * 6,
        scratch_shapes=[pltpu.VMEM(shape, dtype) for _, shape, dtype in NAMES]
        + [pltpu.SemaphoreType.DMA((n,)) for _, n in SEMS],
        compiler_params=pltpu.CompilerParams(
            vmem_limit_bytes=56 * 1024 * 1024, collective_id=0, has_side_effects=True
        ),
    )(
        tokens, cotangent, norm1_gain.reshape(1, C), w_qkv, w_proj,
        bias_table.transpose(0, 2, 1, 3).reshape(12, 1, POS), pos_index, mask_ids,
        norm2_gain.reshape(1, C), w_fc1, w_fc2.T,
    )
    f32 = lambda *shape: jax.ShapeDtypeStruct(shape, F32)
    block, gtok, gn1, gqkv, gproj, gtable, gn2, gfc1, gfc2 = pl.pallas_call(
        finish_kernel,
        out_shape=[main, main, f32(1, C), f32(C, 576), f32(C, C), f32(12, 1, POS), f32(1, C), f32(C, FFN), f32(C, FFN)],
        in_specs=[anywhere] * 6,
        out_specs=[vm] * 9,
        scratch_shapes=[pltpu.VMEM(out.shape, out.dtype) for out in outs]
        + [pltpu.VMEM((C, FFN), F32), pltpu.SemaphoreType.DMA((6,))],
        compiler_params=pltpu.CompilerParams(vmem_limit_bytes=56 * 1024 * 1024),
    )(*outs)
    gtable = gtable.reshape(2, 6, 1, POS).transpose(0, 2, 1, 3)
    return (block, gtok, gn1.reshape(C), gqkv, gproj, gtable, gn2.reshape(C), gfc1, gfc2.T)


def solution(mesh):
    act = P(None, "lat", "lon", None)
    table = P(None, "lat", None, None)
    return jax.shard_map(
        shards,
        mesh=mesh,
        in_specs=(act, P(), P(), P(), table, P(), P("lat"), P(), P(), P(), act),
        out_specs=(act, act, P(), P(), P(), table, P(), P(), P()),
        check_vma=False,
    )
```

```python
import jax
import jax.numpy as jnp
from jax import lax
from jax.experimental import pallas as pl
from jax.experimental.pallas import tpu as pltpu
from jax.sharding import PartitionSpec as P

F32 = jnp.float32
BF16 = jnp.bfloat16
C = 192
HEADS = 6
FFN = 768
WIN = 144
NWIN = 8
TOK = 1152
POS = 3312
EPS = 1e-05
GELU_K = 0.7978845608
GELU_C = 0.044715
LOG2E = 1.4426950408889634
LN2 = 0.6931471805599453
SCALE = 32 ** -0.5
FACTOR = 147456.0 ** -0.5


def nn(a, b):
    return lax.dot_general(a, b, (((1,), (0,)), ((), ())), preferred_element_type=F32)


def nt(a, b):
    return lax.dot_general(a, b, (((1,), (1,)), ((), ())), preferred_element_type=F32)


def tn(a, b):
    return lax.dot_general(a, b, (((0,), (0,)), ((), ())), preferred_element_type=F32)


def head_mask(h, dtype):
    lane = lax.broadcasted_iota(jnp.int32, (1, C), 1)
    inside = (lane >= h * 32) & (lane < h * 32 + 32)
    return jnp.where(inside, 1.0, 0.0).astype(dtype)


def spread_heads(x):
    return jnp.concatenate([x * head_mask(h, BF16) for h in range(HEADS)], axis=0)


def pick_heads(x):
    total = x[:WIN] * head_mask(0, F32)
    for h in range(1, HEADS):
        total = total + x[h * WIN : (h + 1) * WIN] * head_mask(h, F32)
    return total


def mean_of(x):
    return jnp.sum(x, axis=-1, keepdims=True) * (1.0 / C)


def norm_stats(x):
    center = x - mean_of(x)
    inv = lax.rsqrt(mean_of(center * center) + EPS)
    return center * inv, inv


def norm_back(g, normed, inv):
    return inv * (g - mean_of(g) - normed * mean_of(g * normed))


def zone_row(mask_ref, out_ref):
    lane = lax.broadcasted_iota(jnp.int32, (8, 128), 1)
    ids = jnp.zeros((8, 128), jnp.int32)
    for r in range(6):
        ids = jnp.where(lane == r, 2 * mask_ref[r], ids)
    out_ref[...] = ids.astype(F32)


def prep_bias(z, table_ref, idx_ref, zone_ref, bias_ref):
    sub = lax.broadcasted_iota(jnp.int32, (16, 256), 0)
    lane = lax.broadcasted_iota(jnp.int32, (16, 256), 1)
    lane_row = lane // 12
    col = lane - lane_row * 12
    top_i = jnp.where(sub >= 6, 1, 0)
    top_j = jnp.where(lane_row >= 6, 1, 0)
    row_i = sub - 6 * top_i
    row_j = lane_row - 6 * top_j
    zone_i = top_i.astype(F32) if z == 1 else jnp.zeros((16, 256), F32)
    zone_j = top_j.astype(F32) if z == 1 else jnp.zeros((16, 256), F32)
    for r in range(6):
        here = jnp.broadcast_to(zone_ref[0:1, r : r + 1], (16, 256))
        zone_i = zone_i + jnp.where(row_i == r, here, 0.0)
        zone_j = zone_j + jnp.where(row_j == r, here, 0.0)
    mask = jnp.where(zone_i == zone_j, 0.0, -1e30)
    groups = (
        idx_ref[0:8, :],
        idx_ref[16:24, :],
        jnp.concatenate([idx_ref[8:12, :], idx_ref[24:28, :]], axis=0),
    )
    edge = lax.broadcasted_iota(jnp.int32, (8, 128), 1) < 16
    rests = jnp.where(edge, groups[0][:, 128:], 0)
    for g in (1, 2):
        rests = rests + pltpu.roll(jnp.where(edge, groups[g][:, 128:], 0), 16 * g, 1)
    idx = jnp.concatenate([x[:, :128] for x in groups] + [rests], axis=0)
    hi = idx >> 7
    lo = idx & 127

    def one(h, carry):
        row = table_ref[h] * LOG2E
        acc = jnp.zeros((32, 128), F32)
        for a in range(26):
            part = row[:, a * 128 : min(POS, (a + 1) * 128)]
            if a == 25:
                part = jnp.concatenate([part, jnp.zeros((1, 16), F32)], axis=1)
            got = jnp.take_along_axis(jnp.broadcast_to(part, (32, 128)), lo, axis=1)
            acc = jnp.where(hi == a, got, acc)
        rest = acc[24:32]
        wide = [
            jnp.concatenate([acc[8 * g : 8 * g + 8], pltpu.roll(rest, 128 - 16 * g, 1) if g else rest], axis=1)
            for g in range(3)
        ]
        upper = jnp.concatenate([wide[0], wide[2][0:4], wide[2][0:4]], axis=0)
        lower = jnp.concatenate([wide[1], wide[2][4:8], wide[2][4:8]], axis=0)
        for c in range(12):
            ahead = pltpu.roll(upper, c, 1) if c else upper
            val = jnp.where(col >= c, ahead, pltpu.roll(lower, 256 - 12 + c, 1)) + mask
            bias_ref[0, 6 * z + h, pl.ds(c, 12, stride=12), :] = val[:12, :128]
            bias_ref[1, 6 * z + h, pl.ds(c, 12, stride=12), :] = val[:12, 128:]
        return carry

    lax.fori_loop(0, 6, one, 0)


def assemble(ext_ref, win_ref, z):
    for level in (2 * z, 2 * z + 1):
        for r in range(6):
            slab = ext_ref[(level + 1) % 4, r, :, :].astype(F32)
            for w in range(4):
                start = (z * 4 + w) * WIN + ((level % 2) * 6 + r) * 12
                win_ref[start : start + 12, :] = slab[6 + 12 * w : 18 + 12 * w]


def index_rows(pos_ref, idx_ref):
    idx_ref[...] = jnp.zeros_like(idx_ref)
    for lr in range(12):
        idx_ref[lr : lr + 1, 0:WIN] = pos_ref[lr * 12 : lr * 12 + 1, :]
        idx_ref[16 + lr : 17 + lr, 0:WIN] = pos_ref[lr * 12 + 11 : lr * 12 + 12, :]
    idx_ref[16:32, :] = pltpu.roll(idx_ref[16:32, :], 1, 1)


def disassemble(win_ref, slab_ref, ext_ref):
    for level in range(4):
        for r in range(6):
            k = r % 2
            for w in range(4):
                start = ((level // 2) * 4 + w) * WIN + ((level % 2) * 6 + r) * 12
                slab_ref[k, 6 + 12 * w : 18 + 12 * w, :] = win_ref[start : start + 12, :]
            ext_ref[(level + 1) % 4, r, :, :] = slab_ref[k].astype(BF16)


def attention_window(wi, s):
    rows = slice(wi * WIN, (wi + 1) * WIN)
    z = wi // 4
    x = s.x[rows, :]
    normed1, inv1 = norm_stats(x)
    hid = (normed1 * s.n1[...]).astype(BF16)
    s.normed1[rows, :] = normed1
    s.inv1[rows, :] = inv1
    s.hid[rows, :] = hid
    q = (nn(hid, s.wq[0]) * (SCALE * LOG2E)).astype(BF16)
    k = nn(hid, s.wq[1]).astype(BF16)
    v = nn(hid, s.wq[2]).astype(BF16)
    s.k[rows, :] = k
    s.v[rows, :] = v
    qm = spread_heads(q)
    s.q[rows, :] = q
    scores = nt(qm, k)
    b0 = s.bias[0, 6 * z : 6 * z + 6].reshape(864, 128)
    b1 = s.bias[1, 6 * z : 6 * z + 6].reshape(864, 128)
    bias = jnp.concatenate([b0, b1], axis=1)[:, :WIN]
    e = jnp.exp2(scores + bias)
    p = (e * (1.0 / jnp.sum(e, axis=-1, keepdims=True))).astype(BF16)
    s.p[wi] = p
    att = pick_heads(nn(p, v)).astype(BF16)
    s.att[rows, :] = att
    s.blk[rows, :] = x + nn(att, s.wp[...]).astype(BF16).astype(F32)


def mlp_window(wi, s):
    rows = slice(wi * WIN, (wi + 1) * WIN)
    mid = s.blk[rows, :]
    normed2, inv2 = norm_stats(mid)
    hid2 = (normed2 * s.n2[...]).astype(BF16)
    s.hid2[rows, :] = hid2
    pre = nn(hid2, s.w1[...])
    u = pre * pre
    t = jnp.tanh(pre * (GELU_K + (GELU_K * GELU_C) * u))
    half = 0.5 + 0.5 * t
    act = pre * half
    slope = half + act * (1.0 - half) * (2.0 * GELU_K + (6.0 * GELU_K * GELU_C) * u)
    act = act.astype(BF16)
    s.act[rows, :] = act
    s.blk[rows, :] = mid + nt(act, s.w2[...])
    cot = s.cot[rows, :]
    d_act = nn(cot.astype(BF16), s.w2[...])
    d_pre = (d_act * slope).astype(BF16)
    s.d_pre[rows, :] = d_pre
    d_hid2 = nt(d_pre, s.w1[...])
    s.gn[1:2, :] += jnp.sum(d_hid2 * normed2, axis=0, keepdims=True)
    s.d_mid[rows, :] = cot + norm_back(d_hid2 * s.n2[...], normed2, inv2)


def backward_window(wi, s):
    rows = slice(wi * WIN, (wi + 1) * WIN)
    z = wi // 4
    d_mid = s.d_mid[rows, :]
    d_att = nt(d_mid.astype(BF16), s.wp[...]).astype(BF16)
    dom = spread_heads(d_att)
    v = s.v[rows, :]
    p = s.p[wi]
    d_p = nt(dom, v)
    d_v = tn(p, dom).astype(BF16)
    pf = p.astype(F32)
    pd = pf * d_p
    d_s = pd - pf * jnp.sum(pd, axis=-1, keepdims=True)
    d_s0, d_s1 = d_s[:, :128].reshape(6, WIN, 128), d_s[:, 128:].reshape(6, WIN, 16)
    if wi % 4:
        d_s0 = d_s0 + s.d_bias[0, 6 * z : 6 * z + 6]
        d_s1 = d_s1 + s.d_bias[1, 6 * z : 6 * z + 6, :, 0:16]
    s.d_bias[0, 6 * z : 6 * z + 6] = d_s0
    s.d_bias[1, 6 * z : 6 * z + 6, :, 0:16] = d_s1
    d_low = d_s.astype(BF16)
    d_k = (tn(d_low, spread_heads(s.q[rows, :])) * LN2).astype(BF16)
    d_q = (pick_heads(nn(d_low, s.k[rows, :])) * SCALE).astype(BF16)
    s.dq[rows, :] = d_q
    s.dk[rows, :] = d_k
    s.dv[rows, :] = d_v
    d_win = nt(d_q, s.wq[0]) + nt(d_k, s.wq[1]) + nt(d_v, s.wq[2])
    d_hid = d_win.astype(BF16).astype(F32)
    normed1 = s.normed1[rows, :]
    s.gn[0:1, :] += jnp.sum(d_hid * normed1, axis=0, keepdims=True)
    s.x[rows, :] = d_mid + norm_back(d_hid * s.n1[...], normed1, s.inv1[rows, :])


def table_fold(d_bias_ref, can_ref, start, stop):
    lane = lax.broadcasted_iota(jnp.int32, (12, 256), 1)
    col = lane - (lane // 12) * 12

    def one(zh, carry):
        up = jnp.zeros((12, 256), F32)
        down = jnp.zeros((12, 256), F32)
        for c in range(12):
            x0 = d_bias_ref[0, zh, pl.ds(c, 12, stride=12), :]
            x1 = d_bias_ref[1, zh, pl.ds(c, 12, stride=12), :]
            x = jnp.where(lane < WIN, jnp.concatenate([x0, x1], axis=1), 0.0)
            over = jnp.where(col >= c, x, 0.0)
            up = up + (pltpu.roll(over, 256 - c, 1) if c else over)
            if c:
                down = down + pltpu.roll(x - over, 12 - c, 1)
        can_ref[zh, 0:12, :] = up
        can_ref[zh, 12:24, :] = down
        return carry

    lax.fori_loop(start, stop, one, 0)


def table_entries(idx_ref, sums, can_ref, lhs_ref, tab_ref, out_ref):
    can_ref[0:72, 0:128] = sums[0:72]
    for i in range(8):
        can_ref[9 * i : 9 * i + 9, 128:WIN] = sums[72:81, 16 * i : 16 * i + 16]
    entry = lax.broadcasted_iota(jnp.int32, (128, 256), 0)
    lane = lax.broadcasted_iota(jnp.int32, (1, 256), 1)
    spot = lane - (lane // 12) * 12
    acc = jnp.zeros((26 * 8, 128), F32)
    for part in range(2):
        for lr in range(12):
            idx = idx_ref[part * 16 + lr : part * 16 + lr + 1, :]
            ok = lane < WIN
            if part == 1:
                ok = ok & (spot > 0)
            hi = jnp.where(ok, idx >> 7, 99)
            here = jnp.where(entry == (idx & 127), 1.0, 0.0).astype(BF16)
            at = part * 12 + lr
            d = jnp.concatenate([can_ref[24 * k + at : 24 * k + at + 1, :] for k in range(3)] + [jnp.zeros((5, 256), F32)], axis=0)
            for a in range(26):
                lhs_ref[a * 8 : (a + 1) * 8, :] = jnp.where(hi == a, d, 0.0)
            acc = acc + nt(lhs_ref[...].astype(BF16), here)
    for a in range(26):
        tab_ref[3 * a : 3 * a + 3, :] = acc[8 * a : 8 * a + 3]
    out_ref[...] = tab_ref[0:80, :]


class Refs:
    pass


NAMES = [
    ("wq", (3, C, C), BF16),
    ("n1", (1, C), F32),
    ("wqkv", (C, 576), BF16),
    ("wp", (C, C), BF16),
    ("table", (12, 1, POS), F32),
    ("pos", (WIN, WIN), jnp.int32),
    ("n2", (1, C), F32),
    ("w1", (C, FFN), BF16),
    ("w2", (C, FFN), BF16),
    ("bias", (2, 12, WIN, 128), F32),
    ("d_bias", (2, 12, WIN, 128), F32),
    ("x", (TOK, C), F32),
    ("cot", (TOK, C), F32),
    ("blk", (TOK, C), F32),
    ("d_mid", (TOK, C), F32),
    ("normed1", (TOK, C), F32),
    ("inv1", (TOK, 1), F32),
    ("hid", (TOK, C), BF16),
    ("q", (TOK, C), BF16),
    ("k", (TOK, C), BF16),
    ("v", (TOK, C), BF16),
    ("p", (NWIN, 864, WIN), BF16),
    ("att", (TOK, C), BF16),
    ("hid2", (TOK, C), BF16),
    ("act", (TOK, FFN), BF16),
    ("d_pre", (TOK, FFN), BF16),
    ("dq", (TOK, C), BF16),
    ("dk", (TOK, C), BF16),
    ("dv", (TOK, C), BF16),
    ("gn", (8, C), F32),
    ("gall", (C, FFN), F32),
    ("can", (12, 24, 256), F32),
    ("pack", (96, 128), F32),
    ("rest", (72, 16), F32),
    ("idx", (32, 256), jnp.int32),
    ("own_can", (72, 256), F32),
    ("lhs", (26 * 8, 256), F32),
    ("tab", (80, 128), F32),
    ("slab", (2, 64, C), F32),
    ("ext_tok", (4, 6, 64, C), BF16),
    ("ext_cot", (4, 6, 64, C), BF16),
    ("e_blk", (4, 6, 64, C), BF16),
    ("e_tok", (4, 6, 64, C), BF16),
    ("f_own", (2 * C, FFN), BF16),
    ("f_sib", (2 * C, 384), BF16),
    ("f_core", (2 * C, 384), BF16),
    ("f_lat", (8, 48, 384), BF16),
    ("f_lon", (8, 48, 384), BF16),
    ("f_all", (8, 48, 384), BF16),
    ("t_own", (2, 8, 96, 128), BF16),
    ("t_sib", (8, 96, 128), BF16),
    ("t_core", (8, 96, 128), BF16),
    ("t_lon", (8, 96, 128), BF16),
    ("t_lat", (8, 96, 128), BF16),
    ("t_all", (8, 96, 128), BF16),
    ("zone_own", (8, 128), F32),
    ("zone_in", (8, 128), F32),
    ("table_in", (6, 1, POS), F32),
]


def pack_table(s):
    for p in range(12, 16):
        for k in range(3):
            zh = (p - 12) * 3 + k
            s.pack[24 * k : 24 * k + 24, :] = s.can[zh, :, 0:128]
            s.rest[24 * k : 24 * k + 24, :] = s.can[zh, :, 128:WIN]
        for i in range(8):
            s.pack[72:81, 16 * i : 16 * i + 16] = s.rest[9 * i : 9 * i + 9, :]
        s.t_own[p % 2, p // 2, 0:80, :] = s.pack[0:80, :].astype(BF16)
        if p == 12:
            for i in range(2):
                s.pack[88 + 2 * i : 89 + 2 * i, :] = s.gn[i : i + 1, 0:128]
                s.pack[89 + 2 * i : 90 + 2 * i, 0:64] = s.gn[i : i + 1, 128:C]
        else:
            s.pack[88:92, :] = jnp.zeros((4, 128), F32)
        s.t_own[p % 2, p // 2, 80:96, :] = s.pack[80:96, :].astype(BF16)


SEMS = [
    ("local", 24),
    ("in_send", 20),
    ("in_recv", 20),
    ("out_send", 18),
    ("out_recv", 18),
    ("core_send", 5),
    ("core_recv", 5),
] + [(name, 8) for name in ("fa_send", "fa_recv", "fb_send", "fb_recv", "fc_send", "fc_recv")
] + [(name, 16) for name in ("ta_send", "ta_recv", "tb_send", "tb_recv", "tc_send", "tc_recv")]


def remote(src, dst, send, recv, where):
    return pltpu.make_async_remote_copy(
        src_ref=src, dst_ref=dst, send_sem=send, recv_sem=recv, device_id=where, device_id_type=pl.DeviceIdType.MESH
    )


def each_peer(count, me, start, stop, body):
    def one(p, carry):
        @pl.when(p != me)
        def _():
            body(p)

        return carry

    lax.fori_loop(start, stop, one, 0)


def main_kernel(
    tok, cot, n1, wqkv, wp, table, pos, mask, n2, w1, w2,
    blk_main, blk_cols, gtok_main, gtok_cols, f_res, t_res, *scratch
):
    s = Refs()
    for (name, _, _), ref in zip(NAMES, scratch):
        setattr(s, name, ref)
    for (name, _), ref in zip(SEMS, scratch[len(NAMES) :]):
        setattr(s, name, ref)
    fetched = {}
    for i, (name, ref) in enumerate(
        (("pos", pos), ("table", table), ("wqkv", wqkv), ("n1", n1), ("wp", wp), ("n2", n2), ("w1", w1), ("w2", w2))
    ):
        fetched[name] = pltpu.make_async_copy(ref, getattr(s, name), s.local.at[14 + i])
    lon = lax.axis_index("lon")
    lat = lax.axis_index("lat")
    lon_up, lon_down = lax.rem(lon + 1, 16), lax.rem(lon + 15, 16)
    lat_up, lat_down = lax.rem(lat + 1, 8), lax.rem(lat + 7, 8)
    chip = lon // 2
    core = lon - 2 * chip
    sibling = {"lon": lon + 1 - 2 * core, "lat": lat}
    barrier = pltpu.get_barrier_semaphore()
    for name in ("pos", "table", "wqkv"):
        fetched[name].start()

    def greet(a, b):
        pl.semaphore_signal(
            barrier, inc=1, device_id={"lon": a, "lat": b}, device_id_type=pl.DeviceIdType.MESH
        )

    for a in (lon_up, lon_down):
        for b in (lat_down, lat, lat_up):
            greet(a, b)
    each_peer(8, lat, 0, 8, lambda p: greet(lon, p))
    each_peer(8, chip, 0, 8, lambda p: greet(2 * p + core, lat))

    spans = ((1, 3), (3, 4), (0, 1))
    locals_in = []
    halo_in = [[], [], [], []]
    for i, (src, dst) in enumerate(((tok, s.ext_tok), (cot, s.ext_cot))):
        for n, (start, stop) in enumerate(spans):
            kept, gone, far = (slice(3, 6), slice(0, 3), lat_down) if n == 0 else (slice(0, 3), slice(3, 6), lat_up)
            a, b = src.at[start:stop], dst.at[start:stop]
            locals_in.append(pltpu.make_async_copy(a.at[:, kept], b.at[:, gone, 0:48], s.local.at[3 * i + n]))
            moves = (
                (a.at[:, gone], b.at[:, kept, 0:48], {"lon": lon, "lat": far}),
                (a.at[:, kept, 0:16], b.at[:, gone, 48:64], {"lon": lon_down, "lat": lat}),
                (a.at[:, gone, 0:16], b.at[:, kept, 48:64], {"lon": lon_down, "lat": far}),
            )
            for k, (a, b, where) in enumerate(moves):
                at = 9 * i + 3 * n + k
                copy = remote(a, b, s.in_send.at[at], s.in_recv.at[at], where)
                halo_in[2 * i + min(n, 1)].append(copy)
    for copy in locals_in:
        copy.start()
    zone_row(mask, s.zone_own)
    up = {"lon": lon, "lat": lat_up}
    table_copy = remote(table.at[6:12], s.table_in, s.in_send.at[18], s.in_recv.at[18], up)
    zone_copy = remote(s.zone_own, s.zone_in, s.in_send.at[19], s.in_recv.at[19], up)
    pl.semaphore_wait(barrier, 20)
    for copy in halo_in[0] + [zone_copy, table_copy] + halo_in[1]:
        copy.start()

    for name in ("n1", "wp", "n2", "w1", "w2"):
        fetched[name].start()
    fetched["wqkv"].wait()
    for i in range(3):
        s.wq[i] = s.wqkv[:, i * C : (i + 1) * C]
    for ref in (s.gn, s.slab, s.pack, s.own_can, s.tab):
        ref[...] = jnp.zeros_like(ref)
    fetched["pos"].wait()
    index_rows(s.pos, s.idx)
    fetched["table"].wait()
    for name in ("n1", "wp", "n2", "w1", "w2"):
        fetched[name].wait()
    prep_bias(0, s.table, s.idx, s.zone_own, s.bias)

    def arrived(group):
        for copy in halo_in[group]:
            copy.wait_recv()

    def window_loop(body, start, stop):
        for i in range(start, stop):
            body(i, s)

    def send_out(i, e, main, cols):
        copies = []
        for n, (start, stop) in enumerate(spans):
            kept, gone, far = (slice(3, 6), slice(0, 3), lat_up) if n == 0 else (slice(0, 3), slice(3, 6), lat_down)
            a, b, c = e.at[start:stop], main.at[start:stop], cols.at[start:stop]
            copy = pltpu.make_async_copy(a.at[:, gone, 0:48], b.at[:, kept], s.local.at[6 + 3 * i + n])
            copy.start()
            waits = [copy.wait]
            moves = (
                (a.at[:, kept, 0:48], b.at[:, gone], {"lon": lon, "lat": far}),
                (a.at[:, gone, 48:64], c.at[:, kept], {"lon": lon_up, "lat": lat}),
                (a.at[:, kept, 48:64], c.at[:, gone], {"lon": lon_up, "lat": far}),
            )
            for k, (a, b, where) in enumerate(moves):
                at = 9 * i + 3 * n + k
                copy = remote(a, b, s.out_send.at[at], s.out_recv.at[at], where)
                copy.start()
                waits += [copy.wait_send, copy.wait_recv]
            copies += waits
        return copies

    whole = (slice(None), 0)
    parts = ((slice(0, 48), 0), (slice(48, 96), 8))

    def chips_send(src_of, slots, send, recv, start, stop, part=whole):
        rows, at = part

        def go(p):
            where = {"lon": 2 * p + core, "lat": lat}
            remote(src_of(p).at[rows], slots.at[chip, rows], send.at[at + p], recv.at[at + chip], where).start()

        each_peer(8, chip, start, stop, go)

    def chips_wait(src_of, slots, send, recv, part=whole):
        rows, at = part

        def done(p):
            where = {"lon": 2 * p + core, "lat": lat}
            copy = remote(src_of(p).at[rows], slots.at[p, rows], send.at[at + p], recv.at[at + p], where)
            copy.wait_send()
            copy.wait_recv()

        each_peer(8, chip, 0, 8, done)

    def lat_send(src_of, slots, send, recv, part=whole):
        rows, at = part

        def go(p):
            where = {"lon": lon, "lat": p}
            remote(src_of(p).at[rows], slots.at[lat, rows], send.at[at + p], recv.at[at + lat], where).start()

        each_peer(8, lat, 0, 8, go)

    def lat_wait(src_of, slots, send, recv, part=whole):
        rows, at = part

        def done(p):
            where = {"lon": lon, "lat": p}
            copy = remote(src_of(p).at[rows], slots.at[p, rows], send.at[at + p], recv.at[at + p], where)
            copy.wait_send()
            copy.wait_recv()

        each_peer(8, lat, 0, 8, done)

    def half(k):
        return pl.ds(pl.multiple_of(k * 384, 384), 384)

    def core_copy(i, src, dst):
        return remote(src, dst, s.core_send.at[i], s.core_recv.at[i], sibling)

    def f_piece(p):
        return s.f_core.at[pl.ds(pl.multiple_of(p * 48, 48), 48), :]

    def t_piece(p):
        return s.t_core.at[p]

    def f_done(p):
        return s.f_all.at[lat]

    def f_part(p):
        return s.f_lon.at[chip]

    def t_part(p):
        return s.t_lat.at[lat]

    def t_done(p):
        return s.t_all.at[chip]

    def total(slots, count, rows=slice(None)):
        acc = slots[0, rows].astype(F32)
        for i in range(1, count):
            acc = acc + slots[i, rows].astype(F32)
        return acc

    def both(i, s):
        attention_window(i + 4, s)
        mlp_window(i, s)

    for copy in halo_in[2] + halo_in[3]:
        copy.start()
    locals_in[0].wait()
    arrived(0)
    assemble(s.ext_tok, s.x, 0)
    window_loop(attention_window, 0, 4)
    table_copy.wait()
    zone_copy.wait()
    prep_bias(1, s.table_in, s.idx, s.zone_in, s.bias)
    for copy in locals_in[1:3]:
        copy.wait()
    arrived(1)
    assemble(s.ext_tok, s.x, 1)
    locals_in[3].wait()
    arrived(2)
    assemble(s.ext_cot, s.cot, 0)
    window_loop(both, 0, 4)
    for copy in locals_in[4:6]:
        copy.wait()
    arrived(3)
    assemble(s.ext_cot, s.cot, 1)
    window_loop(mlp_window, 4, 8)
    for group in halo_in:
        for copy in group:
            copy.wait_send()
    s.f_own[0:C, :] = tn(s.hid2[...], s.d_pre[...]).astype(BF16)
    s.f_own[C : 2 * C, :] = tn(s.cot[...].astype(BF16), s.act[...]).astype(BF16)
    f_swap = core_copy(0, s.f_own.at[:, half(1 - core)], s.f_sib)
    f_swap.start()
    disassemble(s.blk, s.slab, s.e_blk)
    f_swap.wait()
    s.f_core[...] = (s.f_own[:, half(core)].astype(F32) + s.f_sib[...].astype(F32)).astype(BF16)
    lat_send(f_piece, s.f_lat, s.fa_send, s.fa_recv)
    s.f_lat[lat] = f_piece(lat)[...]

    window_loop(backward_window, 0, 4)
    lat_wait(f_piece, s.f_lat, s.fa_send, s.fa_recv)
    s.f_lon[chip] = total(s.f_lat, 8).astype(BF16)
    chips_send(f_part, s.f_lon, s.fb_send, s.fb_recv, 0, 8)
    out_waits = send_out(0, s.e_blk, blk_main, blk_cols)
    table_fold(s.d_bias, s.can, 0, 6)
    window_loop(backward_window, 4, NWIN)
    chips_wait(f_part, s.f_lon, s.fb_send, s.fb_recv)
    s.f_all[lat] = total(s.f_lon, 8).astype(BF16)
    lat_send(f_done, s.f_all, s.fc_send, s.fc_recv)

    hid = s.hid[...]
    s.gall[:, 0:C] = tn(hid, s.dq[...])
    s.gall[:, C : 2 * C] = tn(hid, s.dk[...])
    s.gall[:, 2 * C : 3 * C] = tn(hid, s.dv[...])
    s.gall[:, 3 * C : 4 * C] = tn(s.att[...], s.d_mid[...].astype(BF16))
    for p in range(12):
        for t in range(6):
            part = s.gall[p * 16 : (p + 1) * 16, t * 128 : (t + 1) * 128]
            s.t_own[p % 2, p // 2, t * 16 : (t + 1) * 16, :] = part.astype(BF16)
    t_swap = core_copy(1, s.t_own.at[1 - core, 0:6], s.t_sib.at[0:6])
    t_swap.start()
    table_fold(s.d_bias, s.can, 6, 12)
    pack_table(s)
    table_swap = core_copy(2, s.t_own.at[1 - core, 6:8], s.t_sib.at[6:8])
    table_swap.start()
    t_swap.wait()
    s.t_core[0:6] = (s.t_own[core, 0:6].astype(F32) + s.t_sib[0:6].astype(F32)).astype(BF16)
    for part in parts:
        chips_send(t_piece, s.t_lon, s.ta_send, s.ta_recv, 0, 6, part)
    table_swap.wait()
    s.t_core[6:8] = (s.t_own[core, 6:8].astype(F32) + s.t_sib[6:8].astype(F32)).astype(BF16)
    for part in parts:
        chips_send(t_piece, s.t_lon, s.ta_send, s.ta_recv, 6, 8, part)
    s.t_lon[chip] = s.t_core[chip]
    disassemble(s.x, s.slab, s.e_tok)
    out_waits += send_out(1, s.e_tok, gtok_main, gtok_cols)
    for part in parts:
        chips_wait(t_piece, s.t_lon, s.ta_send, s.ta_recv, part)
        s.t_lat[lat, part[0]] = total(s.t_lon, 8, part[0]).astype(BF16)
        lat_send(t_part, s.t_lat, s.tb_send, s.tb_recv, part)
    lat_wait(f_done, s.f_all, s.fc_send, s.fc_recv)
    f_back = core_copy(3, s.f_all, f_res.at[core])
    f_back.start()
    f_here = pltpu.make_async_copy(s.f_all, f_res.at[core], s.local.at[12])
    f_here.start()
    for part in parts:
        lat_wait(t_part, s.t_lat, s.tb_send, s.tb_recv, part)

        @pl.when(chip < 6)
        def _():
            s.t_all[chip, part[0]] = total(s.t_lat, 8, part[0]).astype(BF16)
            chips_send(t_done, s.t_all, s.tc_send, s.tc_recv, 0, 8, part)

    @pl.when(chip >= 6)
    def _():
        owner = jnp.where(chip == 7, lat_up, lat)
        table_entries(s.idx, s.t_lat[owner].astype(F32), s.own_can, s.lhs, s.tab, s.pack.at[0:80])
        s.t_all[chip, 0:80] = s.pack[0:80, :].astype(BF16)
        s.t_all[chip, 80:96] = total(s.t_lat, 8, slice(80, 96)).astype(BF16)
        for part in parts:
            chips_send(t_done, s.t_all, s.tc_send, s.tc_recv, 0, 8, part)

    f_back.wait()
    f_here.wait()
    for wait in out_waits:
        wait()
    for part in parts:
        chips_wait(t_done, s.t_all, s.tc_send, s.tc_recv, part)
    t_back = core_copy(4, s.t_all, t_res.at[core])
    t_back.start()
    t_here = pltpu.make_async_copy(s.t_all, t_res.at[core], s.local.at[13])
    t_here.start()
    t_back.wait()
    t_here.wait()


def finish_kernel(
    *refs
):
    far, outs, near, (w_full, sem) = refs[:6], refs[6:15], refs[15:21], refs[21:]
    block, gtok, gn1, gqkv, gproj, gtable, gn2, gfc1, gfc2 = outs
    blk_main, blk_cols, gtok_main, gtok_cols, f_res, t_res = near
    copies = [pltpu.make_async_copy(a, b, sem.at[i]) for i, (a, b) in enumerate(zip(far, near))]
    for copy in copies:
        copy.start()
    copies[4].wait()
    copies[5].wait()
    col = lax.broadcasted_iota(jnp.int32, (16, C), 0)
    for p in range(16):
        out = gfc1 if p < 8 else gfc2
        g, half = (p // 2) % 4, p % 2
        out[g * 48 : (g + 1) * 48, half * 384 : (half + 1) * 384] = f_res[p % 2, p // 2].astype(F32) * FACTOR
    for p in range(12):
        for t in range(6):
            part = t_res[p % 2, p // 2, t * 16 : (t + 1) * 16, :].astype(F32) * FACTOR
            w_full[p * 16 : (p + 1) * 16, t * 128 : (t + 1) * 128] = part
    gqkv[...] = w_full[:, 0:576]
    gproj[...] = w_full[:, 576:768]
    for p in range(12, 16):
        tab = t_res[p % 2, p // 2, 0:80, :].astype(F32) * FACTOR
        for a in range(26):
            width = min(128, POS - a * 128)
            for k in range(3):
                gtable[(p - 12) * 3 + k, :, a * 128 : a * 128 + width] = tab[a * 3 + k : a * 3 + k + 1, 0:width]
    norms = t_res[0, 6, 80:96, :].astype(F32) * FACTOR
    for i, out in enumerate((gn1, gn2)):
        out[:, 0:128] = norms[8 + 2 * i : 9 + 2 * i, :]
        out[:, 128:C] = norms[9 + 2 * i : 10 + 2 * i, 0:64]
    for i in range(4):
        copies[i].wait()
    for main, cols, out in ((blk_main, blk_cols, block), (gtok_main, gtok_cols, gtok)):
        for level in range(4):
            for r in range(6):
                edge = jnp.where(col < 6, cols[level, r].astype(F32), main[level, r, 0:16, :].astype(F32))
                out[level, r, 0:16, :] = edge.astype(BF16)
                out[level, r, 16:48, :] = main[level, r, 16:48, :]


def shards(tokens, norm1_gain, w_qkv, w_proj, bias_table, pos_index, mask_ids, norm2_gain, w_fc1, w_fc2, cotangent):
    vm = pl.BlockSpec(memory_space=pltpu.VMEM)
    anywhere = pl.BlockSpec(memory_space=pl.ANY)
    main = jax.ShapeDtypeStruct((4, 6, 48, C), BF16)
    cols = jax.ShapeDtypeStruct((4, 6, 16, C), BF16)
    outs = pl.pallas_call(
        main_kernel,
        out_shape=[
            main, cols, main, cols,
            jax.ShapeDtypeStruct((2, 8, 48, 384), BF16),
            jax.ShapeDtypeStruct((2, 8, 96, 128), BF16),
        ],
        in_specs=[anywhere] * 7 + [pl.BlockSpec(memory_space=pltpu.SMEM)] + [anywhere] * 3,
        out_specs=[anywhere] * 6,
        scratch_shapes=[pltpu.VMEM(shape, dtype) for _, shape, dtype in NAMES]
        + [pltpu.SemaphoreType.DMA((n,)) for _, n in SEMS],
        compiler_params=pltpu.CompilerParams(
            vmem_limit_bytes=56 * 1024 * 1024, collective_id=0, has_side_effects=True
        ),
    )(
        tokens, cotangent, norm1_gain.reshape(1, C), w_qkv, w_proj,
        bias_table.transpose(0, 2, 1, 3).reshape(12, 1, POS), pos_index, mask_ids,
        norm2_gain.reshape(1, C), w_fc1, w_fc2.T,
    )
    f32 = lambda *shape: jax.ShapeDtypeStruct(shape, F32)
    block, gtok, gn1, gqkv, gproj, gtable, gn2, gfc1, gfc2 = pl.pallas_call(
        finish_kernel,
        out_shape=[main, main, f32(1, C), f32(C, 576), f32(C, C), f32(12, 1, POS), f32(1, C), f32(C, FFN), f32(C, FFN)],
        in_specs=[anywhere] * 6,
        out_specs=[vm] * 9,
        scratch_shapes=[pltpu.VMEM(out.shape, out.dtype) for out in outs]
        + [pltpu.VMEM((C, FFN), F32), pltpu.SemaphoreType.DMA((6,))],
        compiler_params=pltpu.CompilerParams(vmem_limit_bytes=56 * 1024 * 1024),
    )(*outs)
    gtable = gtable.reshape(2, 6, 1, POS).transpose(0, 2, 1, 3)
    return (block, gtok, gn1.reshape(C), gqkv, gproj, gtable, gn2.reshape(C), gfc1, gfc2.T)


def solution(mesh):
    act = P(None, "lat", "lon", None)
    table = P(None, "lat", None, None)
    return jax.shard_map(
        shards,
        mesh=mesh,
        in_specs=(act, P(), P(), P(), table, P(), P("lat"), P(), P(), P(), act),
        out_specs=(act, act, P(), P(), P(), table, P(), P(), P()),
        check_vma=False,
    )
```
